128 devices in a mesh: seq: 16 (over z, x_lo, core), head: 8 (over y, x_hi).
Axes of the slice: x: 4 (x_hi: 2, x_lo: 2; x = x_hi * 2 + x_lo), y: 4, z: 4, core: 2. Of those that a mesh axis runs over, the one named last changes fastest.
Arguments:
- queries: bfloat16 [24576, 2048], P(('seq', 'head')), may hold values from -21 to 21
- keys: bfloat16 [24576, 2048], P(('seq', 'head')), may hold values from -21 to 21
- values: bfloat16 [24576, 2048], P(('seq', 'head')), may hold values from -6 to 6
- out_grad: bfloat16 [24576, 2048], P(('seq', 'head')), may hold values from -6 to 6
- block_list: int32 [64, 7], replicated, may hold values from -1 to 63, as said below
Outputs:
- attention_out: bfloat16 [24576, 2048], P(('seq', 'head'))
- grad_q: bfloat16 [24576, 2048], P(('seq', 'head'))
- grad_k: bfloat16 [24576, 2048], P(('seq', 'head'))
- grad_v: bfloat16 [24576, 2048], P(('seq', 'head'))
The draws below stay inside these ranges and needn't reach their ends.
Inputs may be any that keep to these rules, and one draw needn't show every extreme that they name: `block_list`: row t lists in ascending order the key tiles read by query tile t, then -1 in the remaining entries, and always lists t. A listed tile of another seq index lies within 2 seq indices of t's; over all query tiles of one seq index, at most 2 distinct tiles of any other seq index are listed, and exactly 2 of each seq index one away.
All inputs are finite; a program needn't handle non-finite values.
Results may differ from the reference program's by a relative error of at most 0.025.
Values may be sent and summed in bfloat16 or wider, within the bound.
A program may use at most 192 MiB of HBM per device.

```python
import jax
import jax.numpy as jnp
from jax import lax

HD = 128
HEADS = 16
TILE = 384
TILES_DEV = 4
REACH = 2
CAP = 2
MAXK = 7
TILES = 64
TOKENS = 24576


def draw_queries(key, part):
    key = jax.random.fold_in(key, 5)
    result = jnp.clip(jax.random.normal(key, (TOKENS, HEADS * HD), jnp.float32), -4.0, 4.0)
    return result.astype(jnp.bfloat16)


def draw_keys(key, part):
    key = jax.random.fold_in(key, 6)
    result = jnp.clip(jax.random.normal(key, (TOKENS, HEADS * HD), jnp.float32), -4.0, 4.0)
    return result.astype(jnp.bfloat16)


def draw_block_list(key, part):
    key = jax.random.fold_in(key, 9)
    group = TILES // TILES_DEV
    parts = jax.random.split(key, 5)
    tiles = jnp.arange(TILES, dtype=jnp.int32)
    owner = tiles // TILES_DEV
    place = tiles % TILES_DEV
    devices = jnp.arange(group, dtype=jnp.int32)
    noise = jax.random.randint(parts[0], (group, TILES), 0, 4096) * TILES_DEV + place[None, :]
    same_owner = owner[:, None] == owner[None, :]
    rank = jnp.sum((noise[:, None, :] < noise[:, :, None]) & same_owner[None, :, :], axis=2)
    gap = jnp.abs(owner[None, :] - devices[:, None])
    extra = jax.random.randint(parts[1], (group, group), 1, CAP + 1)
    quota = jnp.where(gap == 1, CAP, extra[:, owner])
    chosen = (gap >= 1) & (gap <= REACH) & (rank < quota)
    chosen_rows = chosen[owner]
    earlier = owner[None, :] < owner[:, None]
    lower = place < TILES_DEV // 2
    side = jnp.where(lower[:, None], earlier, jnp.logical_not(earlier))
    forced = jnp.where(lower, place == 0, place == TILES_DEV - 1)
    level = jax.random.randint(parts[2], (group,), 1, 4)[owner]
    coin = jax.random.randint(parts[3], (TILES, TILES), 0, 4) < level[:, None]
    remote = chosen_rows & side & (forced[:, None] | coin)
    flip = jax.random.randint(parts[4], (TILES, TILES), 0, 2) == 1
    near = same_owner & (jnp.abs(place[:, None] - place[None, :]) == 1) & flip
    listed = remote | near | (tiles[:, None] == tiles[None, :])
    order = jnp.cumsum(listed.astype(jnp.int32), axis=1) - 1
    count = jnp.sum(listed.astype(jnp.int32), axis=1)
    slots = jnp.arange(MAXK, dtype=jnp.int32)
    hit = listed[:, :, None] & (order[:, :, None] == slots[None, None, :])
    entry = jnp.sum(jnp.where(hit, tiles[None, :, None], 0), axis=1)
    return jnp.where(slots[None, :] < count[:, None], entry, -1).astype(jnp.int32)


def block_levels(stream_key, dims, cuts, low, largest):
    level, own = 1.0, jax.random.fold_in(stream_key, 6)
    for dim, blocks in cuts:
        draws = jnp.exp(jax.random.uniform(jax.random.fold_in(own, dim), (blocks,), jnp.float32, low / len(cuts), largest / len(cuts)))
        level = level * jnp.repeat(draws, dims[dim] // blocks).reshape([-1 if axis == dim else 1 for axis in range(len(dims))])
    return level


def gaussian(rng, dims, scale, reach, cuts=(), kind=jnp.bfloat16):
    values = scale * jax.random.normal(rng, dims, jnp.float32)
    if cuts:
        values = values * block_levels(rng, dims, cuts, -0.22, 0.18)
    return jnp.clip(values, -reach, reach).astype(kind)


def setup_inputs(seed: int = 0) -> dict:
    key_of = jax.random.split(jax.random.key(seed), 6)
    queries = draw_queries(jax.random.fold_in(key_of[5], 71), 0)
    keys = draw_keys(jax.random.fold_in(key_of[5], 71), 0)
    values = gaussian(key_of[2], (TOKENS, HEADS * HD), 1.0, 6.0, ((0, 128),))
    out_grad = gaussian(key_of[3], (TOKENS, HEADS * HD), 1.0, 6.0, ((0, 128),))
    block_list = draw_block_list(jax.random.fold_in(key_of[5], 71), 0)
    return {"queries": queries, "keys": keys, "values": values, "out_grad": out_grad, "block_list": block_list}


def round_trip(x):
    return lax.optimization_barrier(x.astype(jnp.bfloat16)).astype(jnp.float32)


def reference(queries, keys, values, out_grad, block_list):
    scale = HD ** -0.5
    group = TILES // TILES_DEV
    span = (2 * REACH + 1) * TILES_DEV
    q_all = queries.reshape(TILES, TILE, HEADS, HD)
    k_all = keys.reshape(TILES, TILE, HEADS, HD)
    v_all = values.reshape(TILES, TILE, HEADS, HD)
    g_all = out_grad.reshape(TILES, TILE, HEADS, HD)

    def per_device(carry, index):
        total_k, total_v = carry
        start = jnp.clip((index - REACH) * TILES_DEV, 0, TILES - span).astype(jnp.int32)
        k_win = lax.dynamic_slice_in_dim(k_all, start, span, 0)
        v_win = lax.dynamic_slice_in_dim(v_all, start, span, 0)
        first = (index * TILES_DEV).astype(jnp.int32)
        q_dev = lax.dynamic_slice_in_dim(q_all, first, TILES_DEV, 0)
        g_dev = lax.dynamic_slice_in_dim(g_all, first, TILES_DEV, 0)
        rows = lax.dynamic_slice_in_dim(block_list, first, TILES_DEV, 0)

        def per_tile(acc, item):
            acc_k, acc_v = acc
            q_tile, g_tile, row = item
            valid = row >= 0
            place = jnp.clip(row - start, 0, span - 1).astype(jnp.int32)
            k_sel = k_win[place]
            v_sel = v_win[place]
            scores = jnp.einsum("ihd,mjhd->himj", q_tile.astype(jnp.float32), k_sel.astype(jnp.float32)) * scale
            scores = jnp.where(valid[None, None, :, None], scores, -1.0e30)
            top = jnp.max(scores, axis=(2, 3), keepdims=True)
            expo = jnp.exp(scores - top)
            prob = expo / jnp.sum(expo, axis=(2, 3), keepdims=True)
            prob_b = prob.astype(jnp.bfloat16)
            out_tile = jnp.einsum("himj,mjhd->ihd", prob_b.astype(jnp.float32), v_sel.astype(jnp.float32)).astype(jnp.bfloat16)
            delta = jnp.sum(g_tile.astype(jnp.float32) * out_tile.astype(jnp.float32), axis=2)
            dprob = jnp.einsum("ihd,mjhd->himj", g_tile.astype(jnp.float32), v_sel.astype(jnp.float32))
            dscore = (prob * (dprob - delta.T[:, :, None, None])).astype(jnp.bfloat16)
            dq_tile = (jnp.einsum("himj,mjhd->ihd", dscore.astype(jnp.float32), k_sel.astype(jnp.float32)) * scale).astype(jnp.bfloat16)
            dk_part = jnp.einsum("himj,ihd->mjhd", dscore.astype(jnp.float32), q_tile.astype(jnp.float32)) * scale
            dv_part = jnp.einsum("himj,ihd->mjhd", prob_b.astype(jnp.float32), g_tile.astype(jnp.float32))
            keep = valid[:, None, None, None]
            acc_k = acc_k.at[place].add(jnp.where(keep, dk_part, 0.0))
            acc_v = acc_v.at[place].add(jnp.where(keep, dv_part, 0.0))
            return (acc_k, acc_v), (out_tile, dq_tile)

        blank = jnp.zeros((span, TILE, HEADS, HD), jnp.float32)
        (win_k, win_v), (out_dev, dq_dev) = lax.scan(per_tile, (blank, blank), (q_dev, g_dev, rows))
        owner = (start + jnp.arange(span, dtype=jnp.int32)) // TILES_DEV
        remote = (owner != index)[:, None, None, None]
        win_k = jnp.where(remote, round_trip(win_k), win_k)
        win_v = jnp.where(remote, round_trip(win_v), win_v)
        total_k = lax.dynamic_update_slice_in_dim(total_k, lax.dynamic_slice_in_dim(total_k, start, span, 0) + win_k, start, 0)
        total_v = lax.dynamic_update_slice_in_dim(total_v, lax.dynamic_slice_in_dim(total_v, start, span, 0) + win_v, start, 0)
        return (total_k, total_v), (out_dev, dq_dev)

    zero_all = jnp.zeros((TILES, TILE, HEADS, HD), jnp.float32)
    (total_k, total_v), (out_all, dq_all) = lax.scan(per_device, (zero_all, zero_all), jnp.arange(group, dtype=jnp.int32))
    width = HEADS * HD
    attention_out = out_all.reshape(TOKENS, width)
    grad_q = dq_all.reshape(TOKENS, width)
    grad_k = total_k.reshape(TOKENS, width).astype(jnp.bfloat16)
    grad_v = total_v.reshape(TOKENS, width).astype(jnp.bfloat16)
    return (attention_out, grad_q, grad_k, grad_v)
```

```python
import functools

import jax
import jax.numpy as jnp
from jax import lax
from jax.experimental import pallas as pl
from jax.experimental.pallas import tpu as pltpu
from jax.sharding import PartitionSpec as P

HD = 128
HEADS = 16
TILE = 384
HALF = TILE // 2
TILES_DEV = 4
MAXK = 7
GROUPS = 16
PAIRS = GROUPS // 2
OWN = 2 * TILES_DEV
SIDE = 6
SLOTS = OWN + 2 * SIDE
SCALE = HD**-0.5
LOG2E = 1.4426950408889634
MESH = pl.DeviceIdType.MESH
VMEM_LIMIT = 56 * 2**20


def place():
    seq, head = lax.axis_index("seq"), lax.axis_index("head")
    z, x_lo, core = seq // 4, (seq // 2) % 2, seq % 2
    y, x_hi = head // 2, head % 2
    return z, y, x_hi, x_lo, core


def device(z, y, x_hi, x_lo, core):
    return (z * 4 + x_lo * 2 + core, y * 2 + x_hi)


def chain_neighbour(step):
    z, y, x_hi, x_lo, core = place()
    pair = (2 * z + core + step + PAIRS) % PAIRS
    return device(pair // 2, y, x_hi, x_lo, pair % 2)


def head_devices():
    z, y, x_hi, x_lo, core = place()
    found = []
    for dy in range(4):
        for dx in range(4):
            to_y, to_x = (y + dy) % 4, (2 * x_hi + x_lo + dx) % 4
            found.append((device(z, to_y, to_x // 2, to_x % 2, x_lo), to_y * 4 + to_x))
    return found


def token_devices():
    z, y, x_hi, x_lo, core = place()
    found = []
    for dy in range(4):
        for dx in range(2):
            for dc in range(2):
                at_y, at_x, at_core = (y + dy) % 4, (x_hi + dx) % 2, (core + dc) % 2
                found.append((device(z, at_y, at_x, core, at_core), at_core * 4 + at_y, at_x))
    return found


def greet(devices, is_self):
    barrier = pltpu.get_barrier_semaphore()
    for i, there in enumerate(devices):
        if i == 0:
            @pl.when(jnp.logical_not(is_self))
            def _():
                pl.semaphore_signal(barrier, inc=1, device_id=there, device_id_type=MESH)
        else:
            pl.semaphore_signal(barrier, inc=1, device_id=there, device_id_type=MESH)
    pl.semaphore_wait(barrier, len(devices) - is_self.astype(jnp.int32))


def listed(rows, seq, tile0):
    def one_row(r, found):
        low, high = found
        for m in range(MAXK):
            at = rows[seq * TILES_DEV + r, m] - tile0
            inside = (at >= 0) & (at < TILES_DEV)
            low = jnp.minimum(low, jnp.where(inside, at, TILES_DEV))
            high = jnp.maximum(high, jnp.where(inside, at, -1))
        return low, high

    return lax.fori_loop(0, TILES_DEV, one_row, (jnp.int32(TILES_DEV), jnp.int32(-1)))


def asked(pair, side):
    first = 2 * pair
    if side == 0:
        a, b = (first - 2 + GROUPS) % GROUPS, (first - 1 + GROUPS) % GROUPS
        return ((a, 0), (b, 0), (b, 1))
    e, f = (first + 2) % GROUPS, (first + 3) % GROUPS
    return ((e, 0), (e, 1), (f, 1))


def bring_kernel(rows, q_in, k_in, v_in, g_in, q_out, k_out, v_out, g_out, k_side, v_side, picked, here_sem, send_sem, recv_sem, side_send, side_recv):
    z, y, x_hi, x_lo, core = place()
    pair = 2 * z + core
    is_self = x_lo == core
    left, right = chain_neighbour(-1), chain_neighbour(1)
    greet([d for d, _, _ in token_devices()] + [left, right], is_self)
    arrays = ((k_in, k_out), (v_in, v_out), (q_in, q_out), (g_in, g_out))
    tile, row = core * 4 + y, x_hi * HALF
    targets = head_devices()

    def block(src, dst, head):
        return (
            src.at[:, pl.ds(pl.multiple_of(head * HD, HD), HD)],
            dst.at[tile, pl.ds(pl.multiple_of(row, HALF), HALF)],
        )

    for n, (src, dst) in enumerate(arrays):
        for i, (there, head) in enumerate(targets):
            piece, landing = block(src, dst, head)
            if i == 0:
                @pl.when(is_self)
                def _():
                    pltpu.make_async_copy(piece, landing, recv_sem.at[n]).start()

                @pl.when(jnp.logical_not(is_self))
                def _():
                    pltpu.make_async_remote_copy(piece, landing, here_sem.at[n], recv_sem.at[n], there, MESH).start()
            else:
                pltpu.make_async_remote_copy(piece, landing, send_sem.at[n], recv_sem.at[n], there, MESH).start()

    picks = []
    for side in range(2):
        for seq, which in asked(pair, side):
            low, high = listed(rows, seq, (2 * pair + which) * TILES_DEV)
            picks.append((side, which * TILES_DEV + jnp.minimum(low, TILES_DEV - 1)))
            picks.append((side, which * TILES_DEV + jnp.maximum(high, 0)))

    side_copies = []
    for n, dst, beside in ((0, k_out, k_side), (1, v_out, v_side)):
        pltpu.make_async_copy(dst, dst, recv_sem.at[n]).wait()
        for i, (side, tile_at) in enumerate(picks):
            picked[side, n, i % SIDE] = dst[tile_at]
        for side, there in ((0, left), (1, right)):
            copy = pltpu.make_async_remote_copy(
                picked.at[side, n],
                beside.at[pl.ds((1 - side) * SIDE, SIDE)],
                side_send.at[side, n],
                side_recv.at[side, n],
                there,
                MESH,
            )
            copy.start()
            side_copies.append(copy)
    for n, dst in ((2, q_out), (3, g_out)):
        pltpu.make_async_copy(dst, dst, recv_sem.at[n]).wait()
    for copy in side_copies:
        copy.wait()
    for n, (src, dst) in enumerate(arrays):
        most = src.at[:, pl.ds(0, (HEADS - 1) * HD)]
        pltpu.make_async_copy(most, most, send_sem.at[n]).wait()

        @pl.when(jnp.logical_not(is_self))
        def _():
            one = src.at[:, pl.ds(0, HD)]
            pltpu.make_async_copy(one, one, here_sem.at[n]).wait()


def dot(a, b, over_a, over_b):
    return lax.dot_general(a, b, (((over_a,), (over_b,)), ((), ())), preferred_element_type=jnp.float32)


def lanes(x, op):
    return functools.reduce(op, [x[:, i * HD : (i + 1) * HD] for i in range(x.shape[1] // HD)])


def attend_kernel(rows, q_ref, k_own, v_own, g_ref, k_beside, v_beside, o_ref, dq_ref, dk_own, dv_own, dk_side, dv_side, k_ref, v_ref, slot_of, count_of, score, expo, dk_acc, dv_acc, load_sem):
    loads = []
    for n, (own, beside, whole) in enumerate(((k_own, k_beside, k_ref), (v_own, v_beside, v_ref))):
        loads.append(pltpu.make_async_copy(own, whole.at[pl.ds(0, OWN)], load_sem.at[n, 0]))
        loads.append(pltpu.make_async_copy(beside, whole.at[pl.ds(OWN, 2 * SIDE)], load_sem.at[n, 1]))
    for load in loads:
        load.start()
    z, y, x_hi, x_lo, core = place()
    pair = 2 * z + core
    first_tile = 2 * pair * TILES_DEV
    lows = []
    for which, step in ((0, -2), (0, -1), (1, -2), (0, 2), (1, 1), (1, 2)):
        seq = 2 * pair + which
        lows.append(listed(rows, seq, (seq + step) * TILES_DEV)[0])

    def find(t, _):
        which = t // TILES_DEV

        def entry(m, count):
            at = rows[first_tile + t, m] - first_tile
            step = (at + 2 * TILES_DEV) // TILES_DEV - 2
            inner = at - step * TILES_DEV
            own = (step == 0) | (step == 1)
            side_slot = jnp.where(
                step == -2, 0 + (inner != lows[0]).astype(jnp.int32),
                jnp.where(
                    step == -1,
                    jnp.where(which == 0, 2 + (inner != lows[1]).astype(jnp.int32), 4 + (inner != lows[2]).astype(jnp.int32)),
                    jnp.where(
                        step == 2,
                        jnp.where(which == 0, 6 + (inner != lows[3]).astype(jnp.int32), 8 + (inner != lows[4]).astype(jnp.int32)),
                        10 + (inner != lows[5]).astype(jnp.int32),
                    ),
                ),
            )
            slot_of[t, m] = jnp.where(own, at, OWN + side_slot)
            return count + (rows[first_tile + t, m] >= 0).astype(jnp.int32)

        count_of[t] = lax.fori_loop(0, MAXK, entry, jnp.int32(0))
        return 0

    lax.fori_loop(0, OWN, find, 0)
    dk_acc[...] = jnp.zeros_like(dk_acc)
    dv_acc[...] = jnp.zeros_like(dv_acc)
    for load in loads:
        load.wait()

    def one_tile(t, _):
        count = count_of[t]
        q, g = q_ref[t], g_ref[t]

        def scores(m, top):
            s = dot(q, k_ref[slot_of[t, m]], 1, 1)
            score[m] = s
            return jnp.maximum(top, lanes(s, jnp.maximum))

        top = lax.fori_loop(0, count, scores, jnp.full((TILE, HD), -jnp.inf, jnp.float32))
        top = jnp.max(top, axis=1, keepdims=True)

        def weigh(m, carry):
            total, out = carry
            e = jnp.exp2((score[m] - top) * (SCALE * LOG2E))
            eb = e.astype(jnp.bfloat16)
            expo[m] = eb
            return total + lanes(e, jnp.add), out + dot(eb, v_ref[slot_of[t, m]], 1, 0)

        blank = jnp.zeros((TILE, HD), jnp.float32)
        total, out = lax.fori_loop(0, count, weigh, (blank, blank))
        inv = 1.0 / jnp.sum(total, axis=1, keepdims=True)
        ob = (out * inv).astype(jnp.bfloat16)
        o_ref[t] = ob
        gf = g.astype(jnp.float32)
        delta = jnp.sum(gf * ob.astype(jnp.float32), axis=1, keepdims=True)
        gn = (gf * inv).astype(jnp.bfloat16)
        qn = (q.astype(jnp.float32) * inv).astype(jnp.bfloat16)

        def back(m, dq):
            slot = slot_of[t, m]
            eb = expo[m]
            ds = (eb.astype(jnp.float32) * (dot(g, v_ref[slot], 1, 1) - delta)).astype(jnp.bfloat16)
            dk_acc[slot] += dot(ds, qn, 0, 0)
            dv_acc[slot] += dot(eb, gn, 0, 0)
            return dq + dot(ds, k_ref[slot], 1, 0)

        dq = lax.fori_loop(0, count, back, blank)
        dq_ref[t] = (dq * (inv * SCALE)).astype(jnp.bfloat16)
        return 0

    lax.fori_loop(0, OWN, one_tile, 0)
    dk_own[...] = dk_acc[pl.ds(0, OWN)] * SCALE
    dv_own[...] = dv_acc[pl.ds(0, OWN)]
    dk_side[...] = (dk_acc[pl.ds(OWN, 2 * SIDE)] * SCALE).astype(jnp.bfloat16)
    dv_side[...] = dv_acc[pl.ds(OWN, 2 * SIDE)].astype(jnp.bfloat16)


def return_kernel(rows, o_in, dq_in, dk_own, dv_own, dk_side, dv_side, o_out, dq_out, dk_out, dv_out, k_got, v_got, total, send_sem, recv_sem, side_send, side_recv):
    z, y, x_hi, x_lo, core = place()
    pair = 2 * z + core
    is_self = x_lo == core
    left, right = chain_neighbour(-1), chain_neighbour(1)
    greet([d for d, _ in head_devices()] + [left, right], is_self)
    side_copies = []
    for n, src, got in ((0, dk_side, k_got), (1, dv_side, v_got)):
        for side, there in ((0, left), (1, right)):
            copy = pltpu.make_async_remote_copy(
                src.at[pl.ds(side * SIDE, SIDE)],
                got.at[pl.ds((1 - side) * SIDE, SIDE)],
                side_send.at[side, n],
                side_recv.at[side, n],
                there,
                MESH,
            )
            copy.start()
            side_copies.append(copy)
    head = y * 4 + 2 * x_hi + x_lo
    targets = token_devices()

    def send(n, src, dst):
        for i, (there, tile, half) in enumerate(targets):
            piece = src.at[tile, pl.ds(pl.multiple_of(half * HALF, HALF), HALF)]
            landing = dst.at[:, pl.ds(pl.multiple_of(head * HD, HD), HD)]
            if i == 0:
                @pl.when(is_self)
                def _():
                    pltpu.make_async_copy(piece, landing, recv_sem.at[n]).start()

                @pl.when(jnp.logical_not(is_self))
                def _():
                    pltpu.make_async_remote_copy(piece, landing, send_sem.at[n, 0], recv_sem.at[n], there, MESH).start()
            else:
                pltpu.make_async_remote_copy(piece, landing, send_sem.at[n, 1], recv_sem.at[n], there, MESH).start()

    send(0, o_in, o_out)
    send(1, dq_in, dq_out)
    for got in (k_got, v_got):
        got[2 * SIDE] = jnp.zeros((TILE, HD), jnp.bfloat16)
    asks = []
    for side in range(2):
        for i, (seq, which) in enumerate(asked(pair, side)):
            low, high = listed(rows, seq, (2 * pair + which) * TILES_DEV)
            asks.append((which, side * SIDE + 2 * i, low, high))
    for n, own, got, dst in ((0, dk_own, k_got, dk_out), (1, dv_own, v_got, dv_out)):
        for copy in side_copies[2 * n : 2 * n + 2]:
            copy.wait_recv()
        for u in range(OWN):
            value = own[u]
            for which, slot, low, high in asks:
                if which == u // TILES_DEV:
                    inner = u % TILES_DEV
                    at = jnp.where(low == inner, slot, jnp.where(high == inner, slot + 1, 2 * SIDE))
                    value = value + got[at].astype(jnp.float32)
            total[n, u] = value.astype(jnp.bfloat16)
        send(2 + n, total.at[n], dst)
    for copy in side_copies:
        copy.wait_send()
    for n, (src, dst) in enumerate(((o_in, o_out), (dq_in, dq_out), (total.at[0], dk_out), (total.at[1], dv_out))):
        pltpu.make_async_copy(dst, dst, recv_sem.at[n]).wait()
        most = dst.at[:, pl.ds(0, (HEADS - 1) * HD)]
        pltpu.make_async_copy(most, most, send_sem.at[n, 1]).wait()

        @pl.when(jnp.logical_not(is_self))
        def _():
            one = dst.at[:, pl.ds(0, HD)]
            pltpu.make_async_copy(one, one, send_sem.at[n, 0]).wait()


def shape(*dims, dtype=jnp.bfloat16):
    return jax.ShapeDtypeStruct(dims, dtype)


def body(queries, keys, values, out_grad, block_list):
    vmem, hbm = pl.BlockSpec(memory_space=pltpu.VMEM), pl.BlockSpec(memory_space=pl.ANY)
    smem = pl.BlockSpec(memory_space=pltpu.SMEM)
    dma = pltpu.SemaphoreType.DMA
    q, k, v, g, k_side, v_side = pl.pallas_call(
        bring_kernel,
        out_shape=(shape(OWN, TILE, HD),) * 4 + (shape(2 * SIDE, TILE, HD),) * 2,
        in_specs=[smem] + [hbm] * 4,
        out_specs=(hbm, vmem, vmem, hbm, hbm, hbm),
        scratch_shapes=[
            pltpu.VMEM((2, 2, SIDE, TILE, HD), jnp.bfloat16),
            dma((4,)), dma((4,)), dma((4,)), dma((2, 2)), dma((2, 2)),
        ],
        compiler_params=pltpu.CompilerParams(collective_id=0, has_side_effects=True, vmem_limit_bytes=VMEM_LIMIT),
    )(block_list, queries, keys, values, out_grad)
    f32 = jnp.float32
    o, dq, dk_own, dv_own, dk_side, dv_side = pl.pallas_call(
        attend_kernel,
        out_shape=(
            shape(OWN, TILE, HD), shape(OWN, TILE, HD),
            shape(OWN, TILE, HD, dtype=f32), shape(OWN, TILE, HD, dtype=f32),
            shape(2 * SIDE, TILE, HD), shape(2 * SIDE, TILE, HD),
        ),
        in_specs=[smem, vmem, hbm, hbm, vmem, hbm, hbm],
        out_specs=(vmem,) * 6,
        scratch_shapes=[
            pltpu.VMEM((SLOTS, TILE, HD), jnp.bfloat16),
            pltpu.VMEM((SLOTS, TILE, HD), jnp.bfloat16),
            pltpu.SMEM((OWN, MAXK), jnp.int32),
            pltpu.SMEM((OWN,), jnp.int32),
            pltpu.VMEM((MAXK, TILE, TILE), f32),
            pltpu.VMEM((MAXK, TILE, TILE), jnp.bfloat16),
            pltpu.VMEM((SLOTS, TILE, HD), f32),
            pltpu.VMEM((SLOTS, TILE, HD), f32),
            dma((2, 2)),
        ],
        compiler_params=pltpu.CompilerParams(vmem_limit_bytes=VMEM_LIMIT),
    )(block_list, q, k, v, g, k_side, v_side)
    return pl.pallas_call(
        return_kernel,
        out_shape=(shape(HALF, HEADS * HD),) * 4,
        in_specs=[smem, hbm, hbm, vmem, vmem, hbm, hbm],
        out_specs=(hbm,) * 4,
        scratch_shapes=[
            pltpu.VMEM((2 * SIDE + 1, TILE, HD), jnp.bfloat16),
            pltpu.VMEM((2 * SIDE + 1, TILE, HD), jnp.bfloat16),
            pltpu.VMEM((2, OWN, TILE, HD), jnp.bfloat16),
            dma((4, 2)), dma((4,)), dma((2, 2)), dma((2, 2)),
        ],
        compiler_params=pltpu.CompilerParams(collective_id=1, has_side_effects=True, vmem_limit_bytes=VMEM_LIMIT),
    )(block_list, o, dq, dk_own, dv_own, dk_side, dv_side)


def solution(mesh):
    tokens = P(("seq", "head"), None)
    return jax.shard_map(
        body,
        mesh=mesh,
        in_specs=(tokens, tokens, tokens, tokens, P()),
        out_specs=(tokens, tokens, tokens, tokens),
        check_vma=False,
    )
```

```python
import functools

import jax
import jax.numpy as jnp
from jax import lax
from jax.experimental import pallas as pl
from jax.experimental.pallas import tpu as pltpu
from jax.sharding import PartitionSpec as P

HD = 128
HEADS = 16
TILE = 384
HALF = TILE // 2
TILES_DEV = 4
MAXK = 7
GROUPS = 16
PAIRS = GROUPS // 2
OWN = 2 * TILES_DEV
SIDE = 6
SLOTS = OWN + 2 * SIDE
SCALE = HD**-0.5
LOG2E = 1.4426950408889634
MESH = pl.DeviceIdType.MESH
VMEM_LIMIT = 60 * 2**20


def place():
    seq, head = lax.axis_index("seq"), lax.axis_index("head")
    z, x_lo, core = seq // 4, (seq // 2) % 2, seq % 2
    y, x_hi = head // 2, head % 2
    return z, y, x_hi, x_lo, core


def device(z, y, x_hi, x_lo, core):
    return (z * 4 + x_lo * 2 + core, y * 2 + x_hi)


def chain_neighbour(step):
    z, y, x_hi, x_lo, core = place()
    pair = (2 * z + core + step + PAIRS) % PAIRS
    return device(pair // 2, y, x_hi, x_lo, pair % 2)


def head_devices():
    z, y, x_hi, x_lo, core = place()
    found = []
    for dy in range(4):
        for dx in range(4):
            to_y, to_x = (y + dy) % 4, (2 * x_hi + x_lo + dx) % 4
            found.append((device(z, to_y, to_x // 2, to_x % 2, x_lo), to_y * 4 + to_x))
    return found


def token_devices():
    z, y, x_hi, x_lo, core = place()
    found = []
    for dy in range(4):
        for dx in range(2):
            for dc in range(2):
                at_y, at_x, at_core = (y + dy) % 4, (x_hi + dx) % 2, (core + dc) % 2
                found.append((device(z, at_y, at_x, core, at_core), at_core * 4 + at_y, at_x))
    return found


def greet(devices, is_self):
    barrier = pltpu.get_barrier_semaphore()
    for i, there in enumerate(devices):
        if i == 0:
            @pl.when(jnp.logical_not(is_self))
            def _():
                pl.semaphore_signal(barrier, inc=1, device_id=there, device_id_type=MESH)
        else:
            pl.semaphore_signal(barrier, inc=1, device_id=there, device_id_type=MESH)
    pl.semaphore_wait(barrier, len(devices) - is_self.astype(jnp.int32))


def listed(rows, seq, tile0):
    def one_row(r, found):
        low, high = found
        for m in range(MAXK):
            at = rows[seq * TILES_DEV + r, m] - tile0
            inside = (at >= 0) & (at < TILES_DEV)
            low = jnp.minimum(low, jnp.where(inside, at, TILES_DEV))
            high = jnp.maximum(high, jnp.where(inside, at, -1))
        return low, high

    return lax.fori_loop(0, TILES_DEV, one_row, (jnp.int32(TILES_DEV), jnp.int32(-1)))


def asked(pair, side):
    first = 2 * pair
    if side == 0:
        a, b = (first - 2 + GROUPS) % GROUPS, (first - 1 + GROUPS) % GROUPS
        return ((a, 0), (b, 0), (b, 1))
    e, f = (first + 2) % GROUPS, (first + 3) % GROUPS
    return ((e, 0), (e, 1), (f, 1))


def dot(a, b, over_a, over_b):
    return lax.dot_general(a, b, (((over_a,), (over_b,)), ((), ())), preferred_element_type=jnp.float32)


def eights(x, op):
    return op(x.reshape(x.shape[0] // 8, 8, x.shape[1]), axis=0)


def fill_tables(rows, pair, slot_of, count_of, own_from, side_from):
    first_tile = 2 * pair * TILES_DEV
    lows = []
    for which, step in ((0, -2), (0, -1), (1, -2), (0, 2), (1, 1), (1, 2)):
        seq = 2 * pair + which
        lows.append(listed(rows, seq, (seq + step) * TILES_DEV)[0])

    def later(inner, low):
        return (inner != low).astype(jnp.int32)

    def find(t, _):
        first = t < TILES_DEV
        count = jnp.int32(0)
        for m in range(MAXK):
            entry = rows[first_tile + t, m]
            valid = entry >= 0
            at = jnp.where(valid, entry - first_tile, 0)
            step = (at + 2 * TILES_DEV) // TILES_DEV - 2
            inner = at - step * TILES_DEV
            near_left = jnp.where(first, 2 + later(inner, lows[1]), 4 + later(inner, lows[2]))
            near_right = jnp.where(first, 6 + later(inner, lows[3]), 8 + later(inner, lows[4]))
            beside = jnp.where(
                step == -2,
                later(inner, lows[0]),
                jnp.where(step == -1, near_left, jnp.where(step == 2, near_right, 10 + later(inner, lows[5]))),
            )
            slot_of[t, m] = jnp.where((step == 0) | (step == 1), at, OWN + beside)
            count = count + valid.astype(jnp.int32)
        count_of[t] = count
        return 0

    lax.fori_loop(0, OWN, find, 0)

    def where_listed(t, slot):
        found = jnp.int32(OWN * MAXK)
        count = count_of[t]
        for m in range(MAXK):
            found = jnp.where((slot_of[t, m] == slot) & (count > m), t * MAXK + m, found)
        return found

    def own(u, _):
        def one(t, _):
            own_from[u, t] = where_listed(t, u)
            return 0

        return lax.fori_loop(0, OWN, one, 0)

    lax.fori_loop(0, OWN, own, 0)

    def side(j, _):
        second = ((j >= 4) & (j < 6)) | (j >= 8)
        start = jnp.where(second, TILES_DEV, 0)

        def one(i, _):
            side_from[j, i] = where_listed(start + i, OWN + j)
            return 0

        return lax.fori_loop(0, TILES_DEV, one, 0)

    lax.fori_loop(0, 2 * SIDE, side, 0)


def kernel(
    rows, q_in, k_in, v_in, g_in, o_out, dq_out, dk_out, dv_out,
    q_own, k_own, v_own, g_own, k_side, v_side, picked, k_all, v_all, score, expo, inv_of, delta_of, terms,
    dv_sum, o_done, dq_done, dk_done, dv_done, part, k_got, v_got,
    slot_of, count_of, own_from, side_from,
    in_send, in_recv, out_send, out_recv, side_send, side_recv, back_send, back_recv,
):
    z, y, x_hi, x_lo, core = place()
    pair = 2 * z + core
    is_self = x_lo == core
    left, right = chain_neighbour(-1), chain_neighbour(1)
    greet([d for d, _, _ in token_devices()] + [left, right], is_self)
    arrays = ((k_in, k_own), (v_in, v_own), (q_in, q_own), (g_in, g_own))
    tile, row = core * 4 + y, pl.multiple_of(x_hi * HALF, HALF)
    targets = head_devices()

    for n, (src, dst) in enumerate(arrays):
        for i, (there, head) in enumerate(targets):
            piece = src.at[:, pl.ds(pl.multiple_of(head * HD, HD), HD)]
            landing = dst.at[tile, pl.ds(row, HALF)]
            if i == 0:
                @pl.when(is_self)
                def _():
                    pltpu.make_async_copy(piece, landing, in_recv.at[n]).start()

                @pl.when(jnp.logical_not(is_self))
                def _():
                    pltpu.make_async_remote_copy(piece, landing, in_send.at[n], in_recv.at[n], there, MESH).start()
            else:
                pltpu.make_async_remote_copy(piece, landing, in_send.at[n], in_recv.at[n], there, MESH).start()

    def arrived(n):
        dst = arrays[n][1]
        pltpu.make_async_copy(dst, dst, in_recv.at[n]).wait()

    fill_tables(rows, pair, slot_of, count_of, own_from, side_from)
    asks, picks = [], []
    for side in range(2):
        for i, (seq, which) in enumerate(asked(pair, side)):
            low, high = listed(rows, seq, (2 * pair + which) * TILES_DEV)
            asks.append((which, side * SIDE + 2 * i, low, high))
            picks.append((side, which * TILES_DEV + jnp.minimum(low, TILES_DEV - 1)))
            picks.append((side, which * TILES_DEV + jnp.maximum(high, 0)))
    terms[OWN * MAXK] = jnp.zeros((TILE, HD), jnp.float32)
    for got in (k_got, v_got):
        got[2 * SIDE] = jnp.zeros((TILE, HD), jnp.bfloat16)

    side_copies = []
    for n, own, beside, whole in ((0, k_own, k_side, k_all), (1, v_own, v_side, v_all)):
        arrived(n)
        for i, (side, tile_at) in enumerate(picks):
            picked[side, n, i % SIDE] = own[tile_at]
        for side, there in ((0, left), (1, right)):
            copy = pltpu.make_async_remote_copy(
                picked.at[side, n],
                beside.at[pl.ds((1 - side) * SIDE, SIDE)],
                side_send.at[side, n],
                side_recv.at[side, n],
                there,
                MESH,
            )
            copy.start()
            side_copies.append(copy)
        for u in range(OWN):
            whole[u] = own[u]

    def beside_arrived(n, beside, whole):
        for copy in side_copies[2 * n : 2 * n + 2]:
            copy.wait_recv()
        for j in range(2 * SIDE):
            whole[OWN + j] = beside[j]

    def tile_at(step):
        return ((core + step // TILES_DEV) % 2) * TILES_DEV + (y + step) % TILES_DEV

    head = y * 4 + 2 * x_hi + x_lo

    def send(n, src, dst, t):
        at_y, at_core = t % TILES_DEV, t // TILES_DEV
        for dx in range(2):
            at_x = (x_hi + dx) % 2
            there = device(z, at_y, at_x, core, at_core)
            piece = src.at[t, pl.ds(pl.multiple_of(at_x * HALF, HALF), HALF)]
            landing = dst.at[:, pl.ds(pl.multiple_of(head * HD, HD), HD)]
            remote = pltpu.make_async_remote_copy(piece, landing, out_send.at[n], out_recv.at[n], there, MESH)
            if dx == 0:
                here = is_self & (at_y == y) & (at_core == core)

                @pl.when(here)
                def _():
                    pltpu.make_async_copy(piece, landing, out_recv.at[n]).start()

                @pl.when(jnp.logical_not(here))
                def _():
                    remote.start()
            else:
                remote.start()

    beside_arrived(0, k_side, k_all)
    arrived(2)

    def weigh(step, _):
        t = tile_at(step)
        q, count = q_own[t], count_of[t]
        top = jnp.full((8, TILE), -jnp.inf, jnp.float32)
        for m in range(MAXK):
            s = dot(k_all[slot_of[t, m]], q, 1, 1)
            score[m] = s
            top = jnp.maximum(top, jnp.where(count > m, eights(s, jnp.max), -jnp.inf))
        top = jnp.max(top, axis=0, keepdims=True)
        total = jnp.zeros((8, TILE), jnp.float32)
        for m in range(MAXK):
            e = jnp.exp2((score[m] - jnp.where(count > m, top, 1e30)) * (SCALE * LOG2E))
            expo[t * MAXK + m] = e.astype(jnp.bfloat16)
            total = total + eights(e, jnp.sum)
        inv_of[t] = 1.0 / jnp.sum(total, axis=0, keepdims=True)
        return 0

    lax.fori_loop(0, OWN, weigh, 0)
    beside_arrived(1, v_side, v_all)
    arrived(3)

    def forward(step, _):
        t = tile_at(step)
        inv = inv_of[t]
        g_across = g_own[t].T.astype(jnp.float32)
        g_scaled = (g_across * inv).astype(jnp.bfloat16)
        out = jnp.zeros((HD, TILE), jnp.float32)
        for m in range(MAXK):
            e = expo[t * MAXK + m]
            out = out + dot(v_all[slot_of[t, m]], e, 0, 0)
            terms[t * MAXK + m] = dot(e, g_scaled, 1, 1)
        out = (out * inv).astype(jnp.bfloat16)
        o_done[t] = out.T
        delta_of[t] = jnp.sum(g_across * out.astype(jnp.float32), axis=0, keepdims=True)
        send(0, o_done, o_out, t)
        return 0

    lax.fori_loop(0, OWN, forward, 0)

    back_copies = []

    def send_back(n, got, scale):
        def one(j, _):
            value = terms[side_from[j, 0]]
            for i in range(1, TILES_DEV):
                value = value + terms[side_from[j, i]]
            part[n, j] = (value * scale).astype(jnp.bfloat16)
            return 0

        lax.fori_loop(0, 2 * SIDE, one, 0)
        for side, there in ((0, left), (1, right)):
            copy = pltpu.make_async_remote_copy(
                part.at[n, pl.ds(side * SIDE, SIDE)],
                got.at[pl.ds((1 - side) * SIDE, SIDE)],
                back_send.at[side, n],
                back_recv.at[side, n],
                there,
                MESH,
            )
            copy.start()
            back_copies.append(copy)

    def own_sum(u):
        value = terms[own_from[u, 0]]
        for t in range(1, OWN):
            value = value + terms[own_from[u, t]]
        return value

    def with_got(value, u, got):
        for which, slot, low, high in asks:
            if which == u // TILES_DEV:
                inner = u % TILES_DEV
                value = value + got[jnp.where(low == inner, slot, jnp.where(high == inner, slot + 1, 2 * SIDE))].astype(jnp.float32)
        return value.astype(jnp.bfloat16)

    send_back(0, v_got, 1.0)

    def own_values(u, _):
        dv_sum[u] = own_sum(u)
        return 0

    lax.fori_loop(0, OWN, own_values, 0)

    def backward(step, _):
        t = tile_at(step)
        g, inv, delta = g_own[t], inv_of[t], delta_of[t]
        q_scaled = (q_own[t].T.astype(jnp.float32) * inv).astype(jnp.bfloat16)
        for m in range(MAXK):
            dp = dot(v_all[slot_of[t, m]], g, 1, 1)
            ds = (expo[t * MAXK + m].astype(jnp.float32) * (dp - delta)).astype(jnp.bfloat16)
            expo[t * MAXK + m] = ds
            terms[t * MAXK + m] = dot(ds, q_scaled, 1, 1)
        return 0

    lax.fori_loop(0, 6, backward, 0)
    for copy in back_copies:
        copy.wait_recv()
    for u in range(OWN):
        dv_done[u] = with_got(dv_sum[u], u, v_got)

    def send_values(step, _):
        send(3, dv_done, dv_out, tile_at(step))
        return 0

    lax.fori_loop(0, OWN, send_values, 0)
    lax.fori_loop(6, OWN, backward, 0)
    send_back(1, k_got, SCALE)

    def query_grads(step, _):
        t = tile_at(step)
        dq = jnp.zeros((HD, TILE), jnp.float32)
        for m in range(MAXK):
            dq = dq + dot(k_all[slot_of[t, m]], expo[t * MAXK + m], 0, 0)
        dq_done[t] = (dq * (inv_of[t] * SCALE)).astype(jnp.bfloat16).T
        send(1, dq_done, dq_out, t)
        return 0

    lax.fori_loop(0, OWN, query_grads, 0)
    for copy in back_copies[2:]:
        copy.wait_recv()
    for u in range(OWN):
        dk_done[u] = with_got(own_sum(u) * SCALE, u, k_got)

    def send_keys(step, _):
        send(2, dk_done, dk_out, tile_at(step))
        return 0

    lax.fori_loop(0, OWN, send_keys, 0)

    for copy in side_copies + back_copies:
        copy.wait_send()
    for n, dst in enumerate((o_out, dq_out, dk_out, dv_out)):
        pltpu.make_async_copy(dst, dst, out_recv.at[n]).wait()
        most = dst.at[:, pl.ds(0, (HEADS - 1) * HD)]

        @pl.when(is_self)
        def _():
            pltpu.make_async_copy(most, most, in_send.at[n]).wait()
            pltpu.make_async_copy(most, most, out_send.at[n]).wait()

        @pl.when(jnp.logical_not(is_self))
        def _():
            pltpu.make_async_copy(dst, dst, in_send.at[n]).wait()
            pltpu.make_async_copy(dst, dst, out_send.at[n]).wait()


def body(queries, keys, values, out_grad, block_list):
    hbm, smem = pl.BlockSpec(memory_space=pl.ANY), pl.BlockSpec(memory_space=pltpu.SMEM)
    dma = pltpu.SemaphoreType.DMA

    def tiles(*dims):
        return pltpu.VMEM((*dims, TILE, HD), jnp.bfloat16)

    def counts(*dims):
        return pltpu.SMEM(dims, jnp.int32)

    f32 = jnp.float32
    return pl.pallas_call(
        kernel,
        out_shape=(jax.ShapeDtypeStruct((HALF, HEADS * HD), jnp.bfloat16),) * 4,
        in_specs=[smem] + [hbm] * 4,
        out_specs=(hbm,) * 4,
        scratch_shapes=[
            tiles(OWN), tiles(OWN), tiles(OWN), tiles(OWN),
            tiles(2 * SIDE), tiles(2 * SIDE), tiles(2, 2, SIDE), tiles(SLOTS), tiles(SLOTS),
            pltpu.VMEM((MAXK, TILE, TILE), f32),
            pltpu.VMEM((OWN * MAXK, TILE, TILE), jnp.bfloat16),
            pltpu.VMEM((OWN, 1, TILE), f32),
            pltpu.VMEM((OWN, 1, TILE), f32),
            pltpu.VMEM((OWN * MAXK + 1, TILE, HD), f32),
            pltpu.VMEM((OWN, TILE, HD), f32),
            tiles(OWN), tiles(OWN), tiles(OWN), tiles(OWN),
            tiles(2, 2 * SIDE), tiles(2 * SIDE + 1), tiles(2 * SIDE + 1),
            counts(OWN, MAXK), counts(OWN), counts(OWN, OWN), counts(2 * SIDE, TILES_DEV),
            dma((4,)), dma((4,)), dma((4,)), dma((4,)), dma((2, 2)), dma((2, 2)), dma((2, 2)), dma((2, 2)),
        ],
        compiler_params=pltpu.CompilerParams(collective_id=0, has_side_effects=True, vmem_limit_bytes=VMEM_LIMIT),
    )(block_list, queries, keys, values, out_grad)


def solution(mesh):
    tokens = P(("seq", "head"), None)
    return jax.shard_map(
        body,
        mesh=mesh,
        in_specs=(tokens, tokens, tokens, tokens, P()),
        out_specs=(tokens, tokens, tokens, tokens),
        check_vma=False,
    )
```

```python
import functools

import jax
import jax.numpy as jnp
from jax import lax
from jax.experimental import pallas as pl
from jax.experimental.pallas import tpu as pltpu
from jax.sharding import PartitionSpec as P

HD = 128
HEADS = 16
TILE = 384
HALF = TILE // 2
TILES_DEV = 4
MAXK = 7
GROUPS = 16
PAIRS = GROUPS // 2
OWN = 2 * TILES_DEV
SIDE = 6
SLOTS = OWN + 2 * SIDE
SCALE = HD**-0.5
LOG2E = 1.4426950408889634
MESH = pl.DeviceIdType.MESH
VMEM_LIMIT = 60 * 2**20


def place():
    seq, head = lax.axis_index("seq"), lax.axis_index("head")
    z, x_lo, core = seq // 4, (seq // 2) % 2, seq % 2
    y, x_hi = head // 2, head % 2
    return z, y, x_hi, x_lo, core


def device(z, y, x_hi, x_lo, core):
    return (z * 4 + x_lo * 2 + core, y * 2 + x_hi)


def sides():
    z, y, x_hi, x_lo, core = place()
    toward = 2 * core - 1
    pair = 2 * z + core
    near, far = 2 * pair + core, 2 * pair + 1 - core
    there = device((z + toward + 4) % 4, y, x_hi, x_lo, 1 - core)
    return there, device(z, y, x_hi, x_lo, 1 - core), near, far, toward


def head_devices():
    z, y, x_hi, x_lo, core = place()
    found = []
    for dy in range(4):
        for dx in range(4):
            to_y, to_x = (y + dy) % 4, (2 * x_hi + x_lo + dx) % 4
            found.append((device(z, to_y, to_x // 2, to_x % 2, x_lo), to_y * 4 + to_x))
    return found


def token_devices():
    z, y, x_hi, x_lo, core = place()
    found = []
    for dy in range(4):
        for dx in range(2):
            for dc in range(2):
                at_y, at_x, at_core = (y + dy) % 4, (x_hi + dx) % 2, (core + dc) % 2
                found.append((device(z, at_y, at_x, core, at_core), at_core * 4 + at_y, at_x))
    return found


def greet(devices, is_self):
    barrier = pltpu.get_barrier_semaphore()
    for i, there in enumerate(devices):
        if i == 0:
            @pl.when(jnp.logical_not(is_self))
            def _():
                pl.semaphore_signal(barrier, inc=1, device_id=there, device_id_type=MESH)
        else:
            pl.semaphore_signal(barrier, inc=1, device_id=there, device_id_type=MESH)
    pl.semaphore_wait(barrier, len(devices) - is_self.astype(jnp.int32))


def listed(rows, seq, of):
    row0, tile0 = (seq + GROUPS) % GROUPS * TILES_DEV, of * TILES_DEV

    def one_row(r, found):
        low, high = found
        for m in range(MAXK):
            at = rows[m, row0 + r] - tile0
            inside = (at >= 0) & (at < TILES_DEV)
            low = jnp.minimum(low, jnp.where(inside, at, TILES_DEV))
            high = jnp.maximum(high, jnp.where(inside, at, -1))
        return low, high

    return lax.fori_loop(0, TILES_DEV, one_row, (jnp.int32(TILES_DEV), jnp.int32(-1)))


def asking(near, far, toward):
    mine = (
        (near, near + toward), (near, near + 2 * toward), (far, near + toward),
        (near, far - toward), (far, far - toward), (far, far - 2 * toward),
    )
    theirs = (
        (near + toward, near), (near + toward, far), (near + 2 * toward, near),
        (far - 2 * toward, far), (far - toward, far), (far - toward, near),
    )
    return mine, theirs


def dot(a, b, over_a, over_b):
    return lax.dot_general(a, b, (((over_a,), (over_b,)), ((), ())), preferred_element_type=jnp.float32)


def eights(x, op):
    return op(x.reshape(x.shape[0] // 8, 8, x.shape[1]), axis=0)


def fill_tables(rows, near, far, toward, mine, slot_of, count_of, own_from, side_from):
    first_tile = jnp.minimum(near, far) * TILES_DEV
    near_tile, far_tile = near * TILES_DEV - first_tile, far * TILES_DEV - first_tile
    lows = [listed(rows, seq, of)[0] for seq, of in mine]

    def find(t, _):
        is_near = t // TILES_DEV == near_tile // TILES_DEV
        count = jnp.int32(0)
        for m in range(MAXK):
            entry = rows[m, first_tile + t]
            valid = entry >= 0
            at = jnp.where(valid, entry, first_tile)
            away = (at // TILES_DEV - near) * toward
            inner = at % TILES_DEV
            slots = [2 * i + (inner != low).astype(jnp.int32) for i, low in enumerate(lows)]
            beside = jnp.where(
                away == 1,
                jnp.where(is_near, slots[0], slots[2]),
                jnp.where(away == 2, slots[1], jnp.where(away == -2, jnp.where(is_near, slots[3], slots[4]), slots[5])),
            )
            slot_of[t, m] = jnp.where((away == 0) | (away == -1), at - first_tile, OWN + beside)
            count = count + valid.astype(jnp.int32)
        count_of[t] = count
        return 0

    lax.fori_loop(0, OWN, find, 0)

    def where_listed(t, slot):
        found = jnp.int32(OWN * MAXK)
        count = count_of[t]
        for m in range(MAXK):
            found = jnp.where((slot_of[t, m] == slot) & (count > m), t * MAXK + m, found)
        return found

    def own(u, _):
        def one(t, _):
            own_from[u, t] = where_listed(t, u)
            return 0

        return lax.fori_loop(0, OWN, one, 0)

    lax.fori_loop(0, OWN, own, 0)

    def side(j, _):
        of_far = ((j >= 4) & (j < 6)) | (j >= 8)
        start = jnp.where(of_far, far_tile, near_tile)

        def one(i, _):
            side_from[j, i] = where_listed(start + i, OWN + j)
            return 0

        return lax.fori_loop(0, TILES_DEV, one, 0)

    lax.fori_loop(0, 2 * SIDE, side, 0)


def kernel(
    rows_in, q_in, k_in, v_in, g_in, o_out, dq_out, dk_out, dv_out,
    q_own, k_own, v_own, g_own, k_side, v_side, picked, k_all, v_all, score, expo, inv_of, delta_of, terms,
    dv_sum, o_done, dq_done, dk_done, dv_done, part, k_got, v_got,
    rows, slot_of, count_of, own_from, side_from,
    rows_sem, in_send, in_recv, out_send, out_recv, side_send, side_recv, back_send, back_recv,
):
    z, y, x_hi, x_lo, core = place()
    is_self = x_lo == core
    z_side, core_side, near, far, toward = sides()
    mine, theirs = asking(near, far, toward)
    rows_copy = pltpu.make_async_copy(rows_in, rows, rows_sem)
    rows_copy.start()
    greet([d for d, _, _ in token_devices()] + [z_side, core_side], is_self)
    arrays = ((k_in, k_own), (q_in, q_own), (v_in, v_own), (g_in, g_own))
    tile, row = core * 4 + y, pl.multiple_of(x_hi * HALF, HALF)
    targets = head_devices()

    for n, (src, dst) in enumerate(arrays):
        for i, (there, head) in enumerate(targets):
            piece = src.at[:, pl.ds(pl.multiple_of(head * HD, HD), HD)]
            landing = dst.at[tile, pl.ds(row, HALF)]
            if i == 0:
                @pl.when(is_self)
                def _():
                    pltpu.make_async_copy(piece, landing, in_recv.at[n]).start()

                @pl.when(jnp.logical_not(is_self))
                def _():
                    pltpu.make_async_remote_copy(piece, landing, in_send.at[n], in_recv.at[n], there, MESH).start()
            else:
                pltpu.make_async_remote_copy(piece, landing, in_send.at[n], in_recv.at[n], there, MESH).start()

    def arrived(n):
        dst = arrays[n][1]
        pltpu.make_async_copy(dst, dst, in_recv.at[n]).wait()

    rows_copy.wait()
    fill_tables(rows, near, far, toward, mine, slot_of, count_of, own_from, side_from)
    near_tile, far_tile = core * TILES_DEV, (1 - core) * TILES_DEV
    asks = []
    for i, (seq, of) in enumerate(theirs):
        low, high = listed(rows, seq, of)
        asks.append((i in (0, 2, 5), 2 * i, low, high))
    terms[OWN * MAXK] = jnp.zeros((TILE, HD), jnp.float32)
    for got in (k_got, v_got):
        got[2 * SIDE] = jnp.zeros((TILE, HD), jnp.bfloat16)

    side_copies = []

    def to_sides(n, own, beside, whole):
        for of_near, slot, low, high in asks:
            start = near_tile if of_near else far_tile
            picked[n, slot] = own[start + jnp.minimum(low, TILES_DEV - 1)]
            picked[n, slot + 1] = own[start + jnp.maximum(high, 0)]
        for side, there in ((0, z_side), (1, core_side)):
            span = pl.ds(side * SIDE, SIDE)
            copy = pltpu.make_async_remote_copy(
                picked.at[n, span], beside.at[span], side_send.at[side, n], side_recv.at[side, n], there, MESH
            )
            copy.start()
            side_copies.append(copy)
        for u in range(OWN):
            whole[u] = own[u]

    def beside_arrived(n, beside, whole):
        for copy in side_copies[2 * n : 2 * n + 2]:
            copy.wait_recv()
        for j in range(2 * SIDE):
            whole[OWN + j] = beside[j]

    def tile_at(step):
        return ((core + step // TILES_DEV) % 2) * TILES_DEV + (y + step) % TILES_DEV

    head = y * 4 + 2 * x_hi + x_lo

    def send(n, src, dst, t):
        at_y, at_core = t % TILES_DEV, t // TILES_DEV
        for dx in range(2):
            at_x = (x_hi + dx) % 2
            there = device(z, at_y, at_x, core, at_core)
            piece = src.at[t, pl.ds(pl.multiple_of(at_x * HALF, HALF), HALF)]
            landing = dst.at[:, pl.ds(pl.multiple_of(head * HD, HD), HD)]
            remote = pltpu.make_async_remote_copy(piece, landing, out_send.at[n], out_recv.at[n], there, MESH)
            if dx == 0:
                here = is_self & (at_y == y) & (at_core == core)

                @pl.when(here)
                def _():
                    pltpu.make_async_copy(piece, landing, out_recv.at[n]).start()

                @pl.when(jnp.logical_not(here))
                def _():
                    remote.start()
            else:
                remote.start()

    def each(start, stop, do):
        def one(step, _):
            do(tile_at(step))
            return 0

        lax.fori_loop(start, stop, one, 0)

    def weigh(t):
        q, count = q_own[t], count_of[t]
        top = jnp.full((8, TILE), -jnp.inf, jnp.float32)
        for m in range(MAXK):
            s = dot(k_all[slot_of[t, m]], q, 1, 1)
            score[m] = s
            top = jnp.maximum(top, jnp.where(count > m, eights(s, jnp.max), -jnp.inf))
        top = jnp.max(top, axis=0, keepdims=True)
        total = jnp.zeros((8, TILE), jnp.float32)
        for m in range(MAXK):
            e = jnp.exp2((score[m] - jnp.where(count > m, top, 1e30)) * (SCALE * LOG2E))
            expo[t * MAXK + m] = e.astype(jnp.bfloat16)
            total = total + eights(e, jnp.sum)
        inv_of[t] = 1.0 / jnp.sum(total, axis=0, keepdims=True)

    def value_terms(t):
        g_scaled = (g_own[t].T.astype(jnp.float32) * inv_of[t]).astype(jnp.bfloat16)
        for m in range(MAXK):
            terms[t * MAXK + m] = dot(expo[t * MAXK + m], g_scaled, 1, 1)

    def output(t):
        out = jnp.zeros((HD, TILE), jnp.float32)
        for m in range(MAXK):
            out = out + dot(v_all[slot_of[t, m]], expo[t * MAXK + m], 0, 0)
        out = (out * inv_of[t]).astype(jnp.bfloat16)
        o_done[t] = out.T
        send(0, o_done, o_out, t)
        delta_of[t] = jnp.sum(g_own[t].T.astype(jnp.float32) * out.astype(jnp.float32), axis=0, keepdims=True)

    def backward(t):
        g, delta = g_own[t], delta_of[t]
        q_scaled = (q_own[t].T.astype(jnp.float32) * inv_of[t]).astype(jnp.bfloat16)
        for m in range(MAXK):
            dp = dot(v_all[slot_of[t, m]], g, 1, 1)
            ds = (expo[t * MAXK + m].astype(jnp.float32) * (dp - delta)).astype(jnp.bfloat16)
            expo[t * MAXK + m] = ds
            terms[t * MAXK + m] = dot(ds, q_scaled, 1, 1)

    def query_grad(t):
        dq = jnp.zeros((HD, TILE), jnp.float32)
        for m in range(MAXK):
            dq = dq + dot(k_all[slot_of[t, m]], expo[t * MAXK + m], 0, 0)
        dq_done[t] = (dq * (inv_of[t] * SCALE)).astype(jnp.bfloat16).T
        send(1, dq_done, dq_out, t)

    back_copies = {}

    def send_back(n, half, got, scale):
        def one(j, _):
            value = terms[side_from[j, 0]]
            for i in range(1, TILES_DEV):
                value = value + terms[side_from[j, i]]
            part[n, j] = (value * scale).astype(jnp.bfloat16)
            return 0

        for side, there, first, count in (((0, z_side, 0, 4), (1, core_side, 6, 2)), ((0, z_side, 4, 2), (1, core_side, 8, 4)))[half]:
            lax.fori_loop(first, first + count, one, 0)
            span = pl.ds(first, count)
            copy = pltpu.make_async_remote_copy(
                part.at[n, span], got.at[span], back_send.at[n, half, side], back_recv.at[n, half, side], there, MESH
            )
            copy.start()
            back_copies[n, half, side] = copy

    def own_sum(u):
        value = terms[own_from[u, 0]]
        for t in range(1, OWN):
            value = value + terms[own_from[u, t]]
        return value

    def finish(n, got, own, done):
        for half in range(2):
            for side in range(2):
                back_copies[n, half, side].wait_recv()
        for of_near_tile, start in ((True, near_tile), (False, far_tile)):
            for inner in range(TILES_DEV):
                value = own(start + inner)
                for of_near, slot, low, high in asks:
                    if of_near == of_near_tile:
                        at = jnp.where(low == inner, slot, jnp.where(high == inner, slot + 1, 2 * SIDE))
                        value = value + got[at].astype(jnp.float32)
                done[start + inner] = value.astype(jnp.bfloat16)

    arrived(0)
    to_sides(0, k_own, k_side, k_all)
    beside_arrived(0, k_side, k_all)
    arrived(1)
    each(0, 5, weigh)
    arrived(2)
    to_sides(1, v_own, v_side, v_all)
    each(5, OWN, weigh)
    arrived(3)
    each(0, TILES_DEV, value_terms)
    send_back(0, 0, v_got, 1.0)
    each(TILES_DEV, OWN, value_terms)
    send_back(0, 1, v_got, 1.0)

    def own_values(u, _):
        dv_sum[u] = own_sum(u)
        return 0

    lax.fori_loop(0, OWN, own_values, 0)
    beside_arrived(1, v_side, v_all)
    each(0, OWN, output)
    each(0, 1, backward)
    finish(0, v_got, lambda u: dv_sum[u], dv_done)
    each(0, OWN, lambda t: send(3, dv_done, dv_out, t))
    each(1, TILES_DEV, backward)
    send_back(1, 0, k_got, SCALE)
    each(TILES_DEV, OWN, backward)
    send_back(1, 1, k_got, SCALE)
    each(0, OWN, query_grad)
    finish(1, k_got, lambda u: own_sum(u) * SCALE, dk_done)
    each(0, OWN, lambda t: send(2, dk_done, dk_out, t))

    for copy in side_copies + list(back_copies.values()):
        copy.wait_send()
    for n, dst in enumerate((o_out, dq_out, dk_out, dv_out)):
        pltpu.make_async_copy(dst, dst, out_recv.at[n]).wait()
        most = dst.at[:, pl.ds(0, (HEADS - 1) * HD)]

        @pl.when(is_self)
        def _():
            pltpu.make_async_copy(most, most, in_send.at[n]).wait()
            pltpu.make_async_copy(most, most, out_send.at[n]).wait()

        @pl.when(jnp.logical_not(is_self))
        def _():
            pltpu.make_async_copy(dst, dst, in_send.at[n]).wait()
            pltpu.make_async_copy(dst, dst, out_send.at[n]).wait()


def hand_over(*refs):
    sources, results, (held, in_sem, out_sem) = refs[:4], refs[4:8], refs[8:]
    ins, outs = [], []
    for n in range(4):
        for i in range(2):
            part = pl.ds(i * HALF // 2, HALF // 2)
            ins.append(pltpu.make_async_copy(sources[n].at[part], held.at[n, part], in_sem.at[n, i]))
            outs.append(pltpu.make_async_copy(held.at[n, part], results[n].at[part], out_sem.at[n, i]))
    for copy in ins:
        copy.start()
    for arriving, leaving in zip(ins, outs):
        arriving.wait()
        leaving.start()
    for copy in outs:
        copy.wait()


def body(queries, keys, values, out_grad, block_list):
    hbm = pl.BlockSpec(memory_space=pl.ANY)
    dma = pltpu.SemaphoreType.DMA

    def tiles(*dims):
        return pltpu.VMEM((*dims, TILE, HD), jnp.bfloat16)

    def counts(*dims):
        return pltpu.SMEM(dims, jnp.int32)

    f32 = jnp.float32
    results = (jax.ShapeDtypeStruct((HALF, HEADS * HD), jnp.bfloat16),) * 4
    found = pl.pallas_call(
        kernel,
        out_shape=results,
        in_specs=[hbm] * 5,
        out_specs=(hbm,) * 4,
        scratch_shapes=[
            tiles(OWN), tiles(OWN), tiles(OWN), tiles(OWN),
            tiles(2 * SIDE), tiles(2 * SIDE), tiles(2, 2 * SIDE), tiles(SLOTS), tiles(SLOTS),
            pltpu.VMEM((MAXK, TILE, TILE), f32),
            pltpu.VMEM((OWN * MAXK, TILE, TILE), jnp.bfloat16),
            pltpu.VMEM((OWN, 1, TILE), f32),
            pltpu.VMEM((OWN, 1, TILE), f32),
            pltpu.VMEM((OWN * MAXK + 1, TILE, HD), f32),
            pltpu.VMEM((OWN, TILE, HD), f32),
            tiles(OWN), tiles(OWN), tiles(OWN), tiles(OWN),
            tiles(2, 2 * SIDE), tiles(2 * SIDE + 1), tiles(2 * SIDE + 1),
            counts(MAXK, 4 * GROUPS), counts(OWN, MAXK), counts(OWN), counts(OWN, OWN), counts(2 * SIDE, TILES_DEV),
            pltpu.SemaphoreType.DMA, dma((4,)), dma((4,)), dma((4,)), dma((4,)),
            dma((2, 2)), dma((2, 2)), dma((2, 2, 2)), dma((2, 2, 2)),
        ],
        compiler_params=pltpu.CompilerParams(collective_id=0, has_side_effects=True, vmem_limit_bytes=VMEM_LIMIT),
    )(block_list.T, queries, keys, values, out_grad)
    return pl.pallas_call(
        hand_over,
        out_shape=results,
        in_specs=[hbm] * 4,
        out_specs=(hbm,) * 4,
        scratch_shapes=[pltpu.VMEM((4, HALF, HEADS * HD), jnp.bfloat16), dma((4, 2)), dma((4, 2))],
    )(*found)


def solution(mesh):
    tokens = P(("seq", "head"), None)
    return jax.shard_map(
        body,
        mesh=mesh,
        in_specs=(tokens, tokens, tokens, tokens, P()),
        out_specs=(tokens, tokens, tokens, tokens),
        check_vma=False,
    )
```

```python
import functools

import jax
import jax.numpy as jnp
from jax import lax
from jax.experimental import pallas as pl
from jax.experimental.pallas import tpu as pltpu
from jax.sharding import PartitionSpec as P

HD = 128
HEADS = 16
TILE = 384
HALF = TILE // 2
TILES_DEV = 4
MAXK = 7
GROUPS = 16
PAIRS = GROUPS // 2
OWN = 2 * TILES_DEV
SIDE = 6
SLOTS = OWN + 2 * SIDE
SCALE = HD**-0.5
LOG2E = 1.4426950408889634
MESH = pl.DeviceIdType.MESH
VMEM_LIMIT = 60 * 2**20


def place():
    seq, head = lax.axis_index("seq"), lax.axis_index("head")
    z, x_lo, core = seq // 4, (seq // 2) % 2, seq % 2
    y, x_hi = head // 2, head % 2
    return z, y, x_hi, x_lo, core


def device(z, y, x_hi, x_lo, core):
    return (z * 4 + x_lo * 2 + core, y * 2 + x_hi)


def sides():
    z, y, x_hi, x_lo, core = place()
    toward = 2 * core - 1
    pair = 2 * z + core
    near, far = 2 * pair + core, 2 * pair + 1 - core
    there = device((z + toward + 4) % 4, y, x_hi, x_lo, 1 - core)
    return there, device(z, y, x_hi, x_lo, 1 - core), near, far, toward


def head_devices():
    z, y, x_hi, x_lo, core = place()
    found = []
    for dy in range(4):
        for dx in range(4):
            to_y, to_x = (y + dy) % 4, (2 * x_hi + x_lo + dx) % 4
            found.append((device(z, to_y, to_x // 2, to_x % 2, x_lo), to_y * 4 + to_x))
    return found


def token_devices():
    z, y, x_hi, x_lo, core = place()
    found = []
    for dy in range(4):
        for dx in range(2):
            for dc in range(2):
                at_y, at_x, at_core = (y + dy) % 4, (x_hi + dx) % 2, (core + dc) % 2
                found.append((device(z, at_y, at_x, core, at_core), at_core * 4 + at_y, at_x))
    return found


def greet(devices, is_self):
    barrier = pltpu.get_barrier_semaphore()
    for i, there in enumerate(devices):
        if i == 0:
            @pl.when(jnp.logical_not(is_self))
            def _():
                pl.semaphore_signal(barrier, inc=1, device_id=there, device_id_type=MESH)
        else:
            pl.semaphore_signal(barrier, inc=1, device_id=there, device_id_type=MESH)
    pl.semaphore_wait(barrier, len(devices) - is_self.astype(jnp.int32))


def listed(rows, seq, of):
    row0, tile0 = (seq + GROUPS) % GROUPS * TILES_DEV, of * TILES_DEV

    def one_row(r, found):
        low, high = found
        for m in range(MAXK):
            at = rows[m, row0 + r] - tile0
            inside = (at >= 0) & (at < TILES_DEV)
            low = jnp.minimum(low, jnp.where(inside, at, TILES_DEV))
            high = jnp.maximum(high, jnp.where(inside, at, -1))
        return low, high

    return lax.fori_loop(0, TILES_DEV, one_row, (jnp.int32(TILES_DEV), jnp.int32(-1)))


def asking(near, far, toward):
    mine = (
        (near, near + toward), (near, near + 2 * toward), (far, near + toward),
        (near, far - toward), (far, far - toward), (far, far - 2 * toward),
    )
    theirs = (
        (near + toward, near), (near + toward, far), (near + 2 * toward, near),
        (far - 2 * toward, far), (far - toward, far), (far - toward, near),
    )
    return mine, theirs


def dot(a, b, over_a, over_b):
    return lax.dot_general(a, b, (((over_a,), (over_b,)), ((), ())), preferred_element_type=jnp.float32)


def eights(x, op):
    return op(x.reshape(x.shape[0] // 8, 8, x.shape[1]), axis=0)


def fill_tables(rows, near, far, toward, mine, slot_of, count_of, own_from, side_from):
    first_tile = jnp.minimum(near, far) * TILES_DEV
    near_tile, far_tile = near * TILES_DEV - first_tile, far * TILES_DEV - first_tile
    lows = [listed(rows, seq, of)[0] for seq, of in mine]

    def find(t, _):
        is_near = t // TILES_DEV == near_tile // TILES_DEV
        count = jnp.int32(0)
        for m in range(MAXK):
            entry = rows[m, first_tile + t]
            valid = entry >= 0
            at = jnp.where(valid, entry, first_tile)
            away = (at // TILES_DEV - near) * toward
            inner = at % TILES_DEV
            slots = [2 * i + (inner != low).astype(jnp.int32) for i, low in enumerate(lows)]
            beside = jnp.where(
                away == 1,
                jnp.where(is_near, slots[0], slots[2]),
                jnp.where(away == 2, slots[1], jnp.where(away == -2, jnp.where(is_near, slots[3], slots[4]), slots[5])),
            )
            slot_of[t, m] = jnp.where((away == 0) | (away == -1), at - first_tile, OWN + beside)
            count = count + valid.astype(jnp.int32)
        count_of[t] = count
        return 0

    lax.fori_loop(0, OWN, find, 0)

    def where_listed(t, slot):
        found = jnp.int32(OWN * MAXK)
        count = count_of[t]
        for m in range(MAXK):
            found = jnp.where((slot_of[t, m] == slot) & (count > m), t * MAXK + m, found)
        return found

    def own(u, _):
        def one(t, _):
            own_from[u, t] = where_listed(t, u)
            return 0

        return lax.fori_loop(0, OWN, one, 0)

    lax.fori_loop(0, OWN, own, 0)

    def side(j, _):
        of_far = ((j >= 4) & (j < 6)) | (j >= 8)
        start = jnp.where(of_far, far_tile, near_tile)

        def one(i, _):
            side_from[j, i] = where_listed(start + i, OWN + j)
            return 0

        return lax.fori_loop(0, TILES_DEV, one, 0)

    lax.fori_loop(0, 2 * SIDE, side, 0)


def kernel(
    rows_in, q_in, k_in, v_in, g_in, o_out, dq_out, dk_out, dv_out,
    q_own, k_own, v_own, g_own, k_side, v_side, picked, k_all, v_all, score, expo, inv_of, delta_of, terms,
    dv_sum, o_done, dq_done, dk_done, dv_done, part, k_got, v_got,
    rows, slot_of, count_of, own_from, side_from,
    rows_sem, in_send, in_recv, out_send, out_recv, side_send, side_recv, back_send, back_recv,
):
    z, y, x_hi, x_lo, core = place()
    is_self = x_lo == core
    z_side, core_side, near, far, toward = sides()
    mine, theirs = asking(near, far, toward)
    rows_copy = pltpu.make_async_copy(rows_in, rows, rows_sem)
    rows_copy.start()
    greet([d for d, _, _ in token_devices()] + [z_side, core_side], is_self)
    arrays = ((k_in, k_own), (q_in, q_own), (v_in, v_own), (g_in, g_own))
    tile, row = core * 4 + y, pl.multiple_of(x_hi * HALF, HALF)
    targets = head_devices()

    for n, (src, dst) in enumerate(arrays):
        for i, (there, head) in enumerate(targets):
            piece = src.at[:, pl.ds(pl.multiple_of(head * HD, HD), HD)]
            landing = dst.at[tile, pl.ds(row, HALF)]
            if i == 0:
                @pl.when(is_self)
                def _():
                    pltpu.make_async_copy(piece, landing, in_recv.at[n]).start()

                @pl.when(jnp.logical_not(is_self))
                def _():
                    pltpu.make_async_remote_copy(piece, landing, in_send.at[n], in_recv.at[n], there, MESH).start()
            else:
                pltpu.make_async_remote_copy(piece, landing, in_send.at[n], in_recv.at[n], there, MESH).start()

    def arrived(n):
        dst = arrays[n][1]
        pltpu.make_async_copy(dst, dst, in_recv.at[n]).wait()

    rows_copy.wait()
    fill_tables(rows, near, far, toward, mine, slot_of, count_of, own_from, side_from)
    near_tile, far_tile = core * TILES_DEV, (1 - core) * TILES_DEV
    asks = []
    for i, (seq, of) in enumerate(theirs):
        low, high = listed(rows, seq, of)
        asks.append((i in (0, 2, 5), 2 * i, low, high))
    terms[OWN * MAXK] = jnp.zeros((TILE, HD), jnp.float32)
    for got in (k_got, v_got):
        got[2 * SIDE] = jnp.zeros((TILE, HD), jnp.bfloat16)

    side_copies = []

    def to_sides(n, own, beside, whole):
        for of_near, slot, low, high in asks:
            start = near_tile if of_near else far_tile
            picked[n, slot] = own[start + jnp.minimum(low, TILES_DEV - 1)]
            picked[n, slot + 1] = own[start + jnp.maximum(high, 0)]
        for side, there in ((0, z_side), (1, core_side)):
            span = pl.ds(side * SIDE, SIDE)
            copy = pltpu.make_async_remote_copy(
                picked.at[n, span], beside.at[span], side_send.at[side, n], side_recv.at[side, n], there, MESH
            )
            copy.start()
            side_copies.append(copy)
        for u in range(OWN):
            whole[u] = own[u]

    def beside_arrived(n, beside, whole):
        for copy in side_copies[2 * n : 2 * n + 2]:
            copy.wait_recv()
        for j in range(2 * SIDE):
            whole[OWN + j] = beside[j]

    def tile_at(step):
        turn = step % TILES_DEV
        away = jnp.where(turn == 0, 2, jnp.where(turn == 3, 0, jnp.where((turn == 1) == (core == 0), 1, 3)))
        return ((core + step // TILES_DEV) % 2) * TILES_DEV + (y + away) % TILES_DEV

    head = y * 4 + 2 * x_hi + x_lo

    def send(n, src, dst, t):
        at_y, at_core = t % TILES_DEV, t // TILES_DEV
        for dx in range(2):
            at_x = (x_hi + dx) % 2
            there = device(z, at_y, at_x, core, at_core)
            piece = src.at[t, pl.ds(pl.multiple_of(at_x * HALF, HALF), HALF)]
            landing = dst.at[:, pl.ds(pl.multiple_of(head * HD, HD), HD)]
            remote = pltpu.make_async_remote_copy(piece, landing, out_send.at[n], out_recv.at[n], there, MESH)
            if dx == 0:
                here = is_self & (at_y == y) & (at_core == core)

                @pl.when(here)
                def _():
                    pltpu.make_async_copy(piece, landing, out_recv.at[n]).start()

                @pl.when(jnp.logical_not(here))
                def _():
                    remote.start()
            else:
                remote.start()

    def each(start, stop, do, by=1):
        def some(turn, _):
            for i in range(by):
                do(tile_at(start + turn * by + i))
            return 0

        lax.fori_loop(0, (stop - start) // by, some, 0)

    def weigh(t):
        q, count = q_own[t], count_of[t]
        top = jnp.full((8, TILE), -jnp.inf, jnp.float32)
        for m in range(MAXK):
            s = dot(k_all[slot_of[t, m]], q, 1, 1)
            score[m] = s
            top = jnp.maximum(top, jnp.where(count > m, eights(s, jnp.max), -jnp.inf))
        top = jnp.max(top, axis=0, keepdims=True)
        total = jnp.zeros((8, TILE), jnp.float32)
        for m in range(MAXK):
            e = jnp.exp2((score[m] - jnp.where(count > m, top, 1e30)) * (SCALE * LOG2E))
            expo[t * MAXK + m] = e.astype(jnp.bfloat16)
            total = total + eights(e, jnp.sum)
        inv_of[t] = 1.0 / jnp.sum(total, axis=0, keepdims=True)

    def row(t):
        return expo[pl.ds(t * MAXK, MAXK)].reshape(MAXK * TILE, TILE)

    def value_terms(t):
        g_scaled = (g_own[t].T.astype(jnp.float32) * inv_of[t]).astype(jnp.bfloat16)
        terms[pl.ds(t * MAXK, MAXK)] = dot(row(t), g_scaled, 1, 1).reshape(MAXK, TILE, HD)

    def output(t):
        out = jnp.zeros((HD, TILE), jnp.float32)
        for m in range(MAXK):
            out = out + dot(v_all[slot_of[t, m]], expo[t * MAXK + m], 0, 0)
        out = (out * inv_of[t]).astype(jnp.bfloat16)
        o_done[t] = out.T
        send(0, o_done, o_out, t)
        delta_of[t] = jnp.sum(g_own[t].T.astype(jnp.float32) * out.astype(jnp.float32), axis=0, keepdims=True)

    def backward(t):
        g, delta = g_own[t], delta_of[t]
        q_scaled = (q_own[t].T.astype(jnp.float32) * inv_of[t]).astype(jnp.bfloat16)
        for m in range(MAXK):
            dp = dot(v_all[slot_of[t, m]], g, 1, 1)
            ds = (expo[t * MAXK + m].astype(jnp.float32) * (dp - delta)).astype(jnp.bfloat16)
            expo[t * MAXK + m] = ds
        terms[pl.ds(t * MAXK, MAXK)] = dot(row(t), q_scaled, 1, 1).reshape(MAXK, TILE, HD)

    def query_grad(t):
        dq = jnp.zeros((HD, TILE), jnp.float32)
        for m in range(MAXK):
            dq = dq + dot(k_all[slot_of[t, m]], expo[t * MAXK + m], 0, 0)
        dq_done[t] = (dq * (inv_of[t] * SCALE)).astype(jnp.bfloat16).T
        send(1, dq_done, dq_out, t)

    back_copies = {}

    def send_back(n, half, got, scale):
        def one(j, _):
            value = terms[side_from[j, 0]]
            for i in range(1, TILES_DEV):
                value = value + terms[side_from[j, i]]
            part[n, j] = (value * scale).astype(jnp.bfloat16)
            return 0

        for side, there, first, count in (((0, z_side, 0, 4), (1, core_side, 6, 2)), ((0, z_side, 4, 2), (1, core_side, 8, 4)))[half]:
            lax.fori_loop(first, first + count, one, 0)
            span = pl.ds(first, count)
            copy = pltpu.make_async_remote_copy(
                part.at[n, span], got.at[span], back_send.at[n, half, side], back_recv.at[n, half, side], there, MESH
            )
            copy.start()
            back_copies[n, half, side] = copy

    def own_sum(u):
        value = terms[own_from[u, 0]]
        for t in range(1, OWN):
            value = value + terms[own_from[u, t]]
        return value

    def finish(n, got, own, done):
        for half in range(2):
            for side in range(2):
                back_copies[n, half, side].wait_recv()
        for of_near_tile, start in ((True, near_tile), (False, far_tile)):
            for inner in range(TILES_DEV):
                value = own(start + inner)
                for of_near, slot, low, high in asks:
                    if of_near == of_near_tile:
                        at = jnp.where(low == inner, slot, jnp.where(high == inner, slot + 1, 2 * SIDE))
                        value = value + got[at].astype(jnp.float32)
                done[start + inner] = value.astype(jnp.bfloat16)

    arrived(0)
    to_sides(0, k_own, k_side, k_all)
    beside_arrived(0, k_side, k_all)
    arrived(1)
    each(0, 5, weigh)
    arrived(2)
    to_sides(1, v_own, v_side, v_all)
    each(5, OWN, weigh)
    arrived(3)
    each(0, TILES_DEV, value_terms, 4)
    send_back(0, 0, v_got, 1.0)
    each(TILES_DEV, OWN, value_terms, 4)
    send_back(0, 1, v_got, 1.0)
    beside_arrived(1, v_side, v_all)
    each(0, OWN, output, 2)

    def own_values(u, _):
        dv_sum[u] = own_sum(u)
        return 0

    lax.fori_loop(0, OWN, own_values, 0)
    each(0, 2, backward, 2)
    finish(0, v_got, lambda u: dv_sum[u], dv_done)
    each(0, OWN, lambda t: send(3, dv_done, dv_out, t))
    each(2, TILES_DEV, backward, 2)
    send_back(1, 0, k_got, SCALE)
    each(TILES_DEV, OWN, backward, 2)
    send_back(1, 1, k_got, SCALE)
    each(0, OWN, query_grad, 2)
    finish(1, k_got, lambda u: own_sum(u) * SCALE, dk_done)
    each(0, OWN, lambda t: send(2, dk_done, dk_out, t))

    for copy in side_copies + list(back_copies.values()):
        copy.wait_send()
    for n, dst in enumerate((o_out, dq_out, dk_out, dv_out)):
        pltpu.make_async_copy(dst, dst, out_recv.at[n]).wait()
        most = dst.at[:, pl.ds(0, (HEADS - 1) * HD)]

        @pl.when(is_self)
        def _():
            pltpu.make_async_copy(most, most, in_send.at[n]).wait()
            pltpu.make_async_copy(most, most, out_send.at[n]).wait()

        @pl.when(jnp.logical_not(is_self))
        def _():
            pltpu.make_async_copy(dst, dst, in_send.at[n]).wait()
            pltpu.make_async_copy(dst, dst, out_send.at[n]).wait()


def hand_over(*refs):
    sources, results, (held, in_sem, out_sem) = refs[:4], refs[4:8], refs[8:]
    ins, outs = [], []
    for n in range(4):
        for i in range(2):
            part = pl.ds(i * HALF // 2, HALF // 2)
            ins.append(pltpu.make_async_copy(sources[n].at[part], held.at[n, part], in_sem.at[n, i]))
            outs.append(pltpu.make_async_copy(held.at[n, part], results[n].at[part], out_sem.at[n, i]))
    for copy in ins:
        copy.start()
    for arriving, leaving in zip(ins, outs):
        arriving.wait()
        leaving.start()
    for copy in outs:
        copy.wait()


def body(queries, keys, values, out_grad, block_list):
    hbm = pl.BlockSpec(memory_space=pl.ANY)
    dma = pltpu.SemaphoreType.DMA

    def tiles(*dims):
        return pltpu.VMEM((*dims, TILE, HD), jnp.bfloat16)

    def counts(*dims):
        return pltpu.SMEM(dims, jnp.int32)

    f32 = jnp.float32
    results = (jax.ShapeDtypeStruct((HALF, HEADS * HD), jnp.bfloat16),) * 4
    found = pl.pallas_call(
        kernel,
        out_shape=results,
        in_specs=[hbm] * 5,
        out_specs=(hbm,) * 4,
        scratch_shapes=[
            tiles(OWN), tiles(OWN), tiles(OWN), tiles(OWN),
            tiles(2 * SIDE), tiles(2 * SIDE), tiles(2, 2 * SIDE), tiles(SLOTS), tiles(SLOTS),
            pltpu.VMEM((MAXK, TILE, TILE), f32),
            pltpu.VMEM((OWN * MAXK, TILE, TILE), jnp.bfloat16),
            pltpu.VMEM((OWN, 1, TILE), f32),
            pltpu.VMEM((OWN, 1, TILE), f32),
            pltpu.VMEM((OWN * MAXK + 1, TILE, HD), f32),
            pltpu.VMEM((OWN, TILE, HD), f32),
            tiles(OWN), tiles(OWN), tiles(OWN), tiles(OWN),
            tiles(2, 2 * SIDE), tiles(2 * SIDE + 1), tiles(2 * SIDE + 1),
            counts(MAXK, 4 * GROUPS), counts(OWN, MAXK), counts(OWN), counts(OWN, OWN), counts(2 * SIDE, TILES_DEV),
            pltpu.SemaphoreType.DMA, dma((4,)), dma((4,)), dma((4,)), dma((4,)),
            dma((2, 2)), dma((2, 2)), dma((2, 2, 2)), dma((2, 2, 2)),
        ],
        compiler_params=pltpu.CompilerParams(collective_id=0, has_side_effects=True, vmem_limit_bytes=VMEM_LIMIT),
    )(block_list.T, queries, keys, values, out_grad)
    return pl.pallas_call(
        hand_over,
        out_shape=results,
        in_specs=[hbm] * 4,
        out_specs=(hbm,) * 4,
        scratch_shapes=[pltpu.VMEM((4, HALF, HEADS * HD), jnp.bfloat16), dma((4, 2)), dma((4, 2))],
    )(*found)


def solution(mesh):
    tokens = P(("seq", "head"), None)
    return jax.shard_map(
        body,
        mesh=mesh,
        in_specs=(tokens, tokens, tokens, tokens, P()),
        out_specs=(tokens, tokens, tokens, tokens),
        check_vma=False,
    )
```

```python
import functools

import jax
import jax.numpy as jnp
from jax import lax
from jax.experimental import pallas as pl
from jax.experimental.pallas import tpu as pltpu
from jax.sharding import PartitionSpec as P

HD = 128
HEADS = 16
TILE = 384
HALF = TILE // 2
TILES_DEV = 4
MAXK = 7
GROUPS = 16
PAIRS = GROUPS // 2
OWN = 2 * TILES_DEV
SIDE = 6
SLOTS = OWN + 2 * SIDE
SCALE = HD**-0.5
LOG2E = 1.4426950408889634
MESH = pl.DeviceIdType.MESH
VMEM_LIMIT = 60 * 2**20


def place():
    seq, head = lax.axis_index("seq"), lax.axis_index("head")
    z, x_lo, core = seq // 4, (seq // 2) % 2, seq % 2
    y, x_hi = head // 2, head % 2
    return z, y, x_hi, x_lo, core


def device(z, y, x_hi, x_lo, core):
    return (z * 4 + x_lo * 2 + core, y * 2 + x_hi)


def sides():
    z, y, x_hi, x_lo, core = place()
    toward = 2 * core - 1
    pair = 2 * z + core
    near, far = 2 * pair + core, 2 * pair + 1 - core
    there = device((z + toward + 4) % 4, y, x_hi, x_lo, 1 - core)
    return there, device(z, y, x_hi, x_lo, 1 - core), near, far, toward


def turns(step, core):
    return jnp.where(step == 0, 2, jnp.where(step == 3, 0, jnp.where((step == 1) == (core == 0), 1, 3)))


def head_devices():
    z, y, x_hi, x_lo, core = place()
    found = []
    for dy in range(4):
        for dx in range(4):
            to_y, to_x = (y + dy) % 4, (2 * x_hi + x_lo + dx) % 4
            found.append((device(z, to_y, to_x // 2, to_x % 2, x_lo), to_y * 4 + to_x))
    return found


def token_devices():
    z, y, x_hi, x_lo, core = place()
    found = []
    for dy in range(4):
        for dx in range(2):
            for dc in range(2):
                at_y, at_x, at_core = (y + dy) % 4, (x_hi + dx) % 2, (core + dc) % 2
                found.append((device(z, at_y, at_x, core, at_core), at_core * 4 + at_y, at_x))
    return found


def greet(devices, is_self):
    barrier = pltpu.get_barrier_semaphore()
    for i, there in enumerate(devices):
        if i == 0:
            @pl.when(jnp.logical_not(is_self))
            def _():
                pl.semaphore_signal(barrier, inc=1, device_id=there, device_id_type=MESH)
        else:
            pl.semaphore_signal(barrier, inc=1, device_id=there, device_id_type=MESH)
    pl.semaphore_wait(barrier, len(devices) - is_self.astype(jnp.int32))


def listed(rows, seq, of):
    row0, tile0 = (seq + GROUPS) % GROUPS * TILES_DEV, of * TILES_DEV

    def one_row(r, found):
        low, high = found
        for m in range(MAXK):
            at = rows[m, row0 + r] - tile0
            inside = (at >= 0) & (at < TILES_DEV)
            low = jnp.minimum(low, jnp.where(inside, at, TILES_DEV))
            high = jnp.maximum(high, jnp.where(inside, at, -1))
        return low, high

    return lax.fori_loop(0, TILES_DEV, one_row, (jnp.int32(TILES_DEV), jnp.int32(-1)))


def asking(near, far, toward):
    mine = (
        (near, near + toward), (near, near + 2 * toward), (far, near + toward),
        (near, far - toward), (far, far - toward), (far, far - 2 * toward),
    )
    theirs = (
        (near + toward, near), (near + toward, far), (near + 2 * toward, near),
        (far - 2 * toward, far), (far - toward, far), (far - toward, near),
    )
    return mine, theirs


def dot(a, b, over_a, over_b):
    return lax.dot_general(a, b, (((over_a,), (over_b,)), ((), ())), preferred_element_type=jnp.float32)


def eights(x, op):
    return op(x.reshape(x.shape[0] // 8, 8, x.shape[1]), axis=0)


def fill_tables(rows, near, far, toward, mine, slot_of, count_of, own_from, side_from):
    first_tile = jnp.minimum(near, far) * TILES_DEV
    near_tile, far_tile = near * TILES_DEV - first_tile, far * TILES_DEV - first_tile
    lows = [listed(rows, seq, of)[0] for seq, of in mine]

    def find(t, _):
        is_near = t // TILES_DEV == near_tile // TILES_DEV
        count = jnp.int32(0)
        for m in range(MAXK):
            entry = rows[m, first_tile + t]
            valid = entry >= 0
            at = jnp.where(valid, entry, first_tile)
            away = (at // TILES_DEV - near) * toward
            inner = at % TILES_DEV
            slots = [2 * i + (inner != low).astype(jnp.int32) for i, low in enumerate(lows)]
            beside = jnp.where(
                away == 1,
                jnp.where(is_near, slots[0], slots[2]),
                jnp.where(away == 2, slots[1], jnp.where(away == -2, jnp.where(is_near, slots[3], slots[4]), slots[5])),
            )
            slot_of[t, m] = jnp.where((away == 0) | (away == -1), at - first_tile, OWN + beside)
            count = count + valid.astype(jnp.int32)
        count_of[t] = count
        return 0

    lax.fori_loop(0, OWN, find, 0)

    def where_listed(t, slot):
        found = jnp.int32(OWN * MAXK)
        count = count_of[t]
        for m in range(MAXK):
            found = jnp.where((slot_of[t, m] == slot) & (count > m), t * MAXK + m, found)
        return found

    def own(u, _):
        def one(t, _):
            own_from[u, t] = where_listed(t, u)
            return 0

        return lax.fori_loop(0, OWN, one, 0)

    lax.fori_loop(0, OWN, own, 0)

    def side(j, _):
        of_far = ((j >= 4) & (j < 6)) | (j >= 8)
        start = jnp.where(of_far, far_tile, near_tile)

        def one(i, _):
            side_from[j, i] = where_listed(start + i, OWN + j)
            return 0

        return lax.fori_loop(0, TILES_DEV, one, 0)

    lax.fori_loop(0, 2 * SIDE, side, 0)


def kernel(
    rows_in, q_in, k_in, v_in, g_in, o_out, dq_out, dk_out, dv_out,
    q_own, k_own, v_own, g_own, g_0, g_1, g_2, g_3, k_side, v_side, picked, k_all, v_all, score, expo, inv_of, delta_of, terms,
    dv_sum, o_done, dq_done, dk_done, dv_done, part, k_got, v_got,
    rows, slot_of, count_of, own_from, side_from,
    rows_sem, in_send, in_recv, part_recv, out_send, out_recv, side_send, side_recv, back_send, back_recv,
):
    z, y, x_hi, x_lo, core = place()
    is_self = x_lo == core
    z_side, core_side, near, far, toward = sides()
    mine, theirs = asking(near, far, toward)
    rows_copy = pltpu.make_async_copy(rows_in, rows, rows_sem)
    rows_copy.start()
    greet([d for d, _, _ in token_devices()] + [z_side, core_side], is_self)
    arrays = ((k_in, k_own), (q_in, q_own), (v_in, v_own), (g_in, g_own))
    tile, row = core * 4 + y, pl.multiple_of(x_hi * HALF, HALF)
    targets = head_devices()
    g_parts = (g_0, g_1, g_2, g_3)

    for n, (src, dst) in enumerate(arrays):
        for i, (there, head) in enumerate(targets):
            piece = src.at[:, pl.ds(pl.multiple_of(head * HD, HD), HD)]
            landing = g_parts[i // 4].at[core, pl.ds(row, HALF)] if n == 3 else dst.at[tile, pl.ds(row, HALF)]
            sem = part_recv.at[i // 4] if n == 3 else in_recv.at[n]
            if i == 0:
                @pl.when(is_self)
                def _():
                    pltpu.make_async_copy(piece, landing, sem).start()

                @pl.when(jnp.logical_not(is_self))
                def _():
                    pltpu.make_async_remote_copy(piece, landing, in_send.at[n], sem, there, MESH).start()
            else:
                pltpu.make_async_remote_copy(piece, landing, in_send.at[n], sem, there, MESH).start()

    def arrived(n):
        dst = arrays[n][1]
        pltpu.make_async_copy(dst, dst, in_recv.at[n]).wait()

    rows_copy.wait()
    fill_tables(rows, near, far, toward, mine, slot_of, count_of, own_from, side_from)
    near_tile, far_tile = core * TILES_DEV, (1 - core) * TILES_DEV
    asks = []
    for i, (seq, of) in enumerate(theirs):
        low, high = listed(rows, seq, of)
        asks.append((i in (0, 2, 5), 2 * i, low, high))
    terms[OWN * MAXK] = jnp.zeros((TILE, HD), jnp.float32)
    for got in (k_got, v_got):
        got[2 * SIDE] = jnp.zeros((TILE, HD), jnp.bfloat16)

    side_copies = []

    def to_sides(n, own, beside, whole):
        for of_near, slot, low, high in asks:
            start = near_tile if of_near else far_tile
            picked[n, slot] = own[start + jnp.minimum(low, TILES_DEV - 1)]
            picked[n, slot + 1] = own[start + jnp.maximum(high, 0)]
        for side, there in ((0, z_side), (1, core_side)):
            span = pl.ds(side * SIDE, SIDE)
            copy = pltpu.make_async_remote_copy(
                picked.at[n, span], beside.at[span], side_send.at[side, n], side_recv.at[side, n], there, MESH
            )
            copy.start()
            side_copies.append(copy)
        for u in range(OWN):
            whole[u] = own[u]

    def beside_arrived(n, beside, whole):
        for copy in side_copies[2 * n : 2 * n + 2]:
            copy.wait_recv()
        for j in range(2 * SIDE):
            whole[OWN + j] = beside[j]

    def tile_at(step):
        return ((core + step // TILES_DEV) % 2) * TILES_DEV + (y + turns(step % TILES_DEV, core)) % TILES_DEV

    head = y * 4 + 2 * x_hi + x_lo

    def send(n, src, dst, t):
        at_y, at_core = t % TILES_DEV, t // TILES_DEV
        for dx in range(2):
            at_x = (x_hi + dx) % 2
            there = device(z, at_y, at_x, core, at_core)
            piece = src.at[t, pl.ds(pl.multiple_of(at_x * HALF, HALF), HALF)]
            landing = dst.at[:, pl.ds(pl.multiple_of(head * HD, HD), HD)]
            remote = pltpu.make_async_remote_copy(piece, landing, out_send.at[n], out_recv.at[n], there, MESH)
            if dx == 0:
                here = is_self & (at_y == y) & (at_core == core)

                @pl.when(here)
                def _():
                    pltpu.make_async_copy(piece, landing, out_recv.at[n]).start()

                @pl.when(jnp.logical_not(here))
                def _():
                    remote.start()
            else:
                remote.start()

    def each(start, stop, do, by=1):
        def some(turn, _):
            for i in range(by):
                do(tile_at(start + turn * by + i))
            return 0

        lax.fori_loop(0, (stop - start) // by, some, 0)

    def weigh(t):
        q, count = q_own[t], count_of[t]
        top = jnp.full((8, TILE), -jnp.inf, jnp.float32)
        for m in range(MAXK):
            s = dot(k_all[slot_of[t, m]], q, 1, 1)
            score[m] = s
            top = jnp.maximum(top, jnp.where(count > m, eights(s, jnp.max), -jnp.inf))
        top = jnp.max(top, axis=0, keepdims=True)
        total = jnp.zeros((8, TILE), jnp.float32)
        for m in range(MAXK):
            e = jnp.exp2((score[m] - jnp.where(count > m, top, 1e30)) * (SCALE * LOG2E))
            expo[t * MAXK + m] = e.astype(jnp.bfloat16)
            total = total + eights(e, jnp.sum)
        inv_of[t] = 1.0 / jnp.sum(total, axis=0, keepdims=True)

    def row(t):
        return expo[pl.ds(t * MAXK, MAXK)].reshape(MAXK * TILE, TILE)

    def value_terms(t, g):
        g_scaled = (g.T.astype(jnp.float32) * inv_of[t]).astype(jnp.bfloat16)
        terms[pl.ds(t * MAXK, MAXK)] = dot(row(t), g_scaled, 1, 1).reshape(MAXK, TILE, HD)

    def output(t):
        out = jnp.zeros((HD, TILE), jnp.float32)
        for m in range(MAXK):
            out = out + dot(v_all[slot_of[t, m]], expo[t * MAXK + m], 0, 0)
        out = (out * inv_of[t]).astype(jnp.bfloat16)
        o_done[t] = out.T
        send(0, o_done, o_out, t)
        delta_of[t] = jnp.sum(g_own[t].T.astype(jnp.float32) * out.astype(jnp.float32), axis=0, keepdims=True)

    def backward(t):
        g, delta = g_own[t], delta_of[t]
        q_scaled = (q_own[t].T.astype(jnp.float32) * inv_of[t]).astype(jnp.bfloat16)
        for m in range(MAXK):
            dp = dot(v_all[slot_of[t, m]], g, 1, 1)
            ds = (expo[t * MAXK + m].astype(jnp.float32) * (dp - delta)).astype(jnp.bfloat16)
            expo[t * MAXK + m] = ds
        terms[pl.ds(t * MAXK, MAXK)] = dot(row(t), q_scaled, 1, 1).reshape(MAXK, TILE, HD)

    def query_grad(t):
        dq = jnp.zeros((HD, TILE), jnp.float32)
        for m in range(MAXK):
            dq = dq + dot(k_all[slot_of[t, m]], expo[t * MAXK + m], 0, 0)
        dq_done[t] = (dq * (inv_of[t] * SCALE)).astype(jnp.bfloat16).T
        send(1, dq_done, dq_out, t)

    back_copies = {}

    def send_back(n, half, got, scale):
        def one(j, _):
            value = terms[side_from[j, 0]]
            for i in range(1, TILES_DEV):
                value = value + terms[side_from[j, i]]
            part[n, j] = (value * scale).astype(jnp.bfloat16)
            return 0

        for side, there, first, count in (((0, z_side, 0, 4), (1, core_side, 6, 2)), ((0, z_side, 4, 2), (1, core_side, 8, 4)))[half]:
            lax.fori_loop(first, first + count, one, 0)
            span = pl.ds(first, count)
            copy = pltpu.make_async_remote_copy(
                part.at[n, span], got.at[span], back_send.at[n, half, side], back_recv.at[n, half, side], there, MESH
            )
            copy.start()
            back_copies[n, half, side] = copy

    def own_sum(u):
        value = terms[own_from[u, 0]]
        for t in range(1, OWN):
            value = value + terms[own_from[u, t]]
        return value

    def finish(n, got, own, done):
        for half in range(2):
            for side in range(2):
                back_copies[n, half, side].wait_recv()
        for of_near_tile, start in ((True, near_tile), (False, far_tile)):
            for inner in range(TILES_DEV):
                value = own(start + inner)
                for of_near, slot, low, high in asks:
                    if of_near == of_near_tile:
                        at = jnp.where(low == inner, slot, jnp.where(high == inner, slot + 1, 2 * SIDE))
                        value = value + got[at].astype(jnp.float32)
                done[start + inner] = value.astype(jnp.bfloat16)

    arrived(0)
    to_sides(0, k_own, k_side, k_all)
    beside_arrived(0, k_side, k_all)
    arrived(1)
    each(0, 5, weigh)
    arrived(2)
    to_sides(1, v_own, v_side, v_all)
    each(5, OWN, weigh)

    for away, landed in enumerate(g_parts):
        pltpu.make_async_copy(landed, landed, part_recv.at[away]).wait()
        for half in range(2):
            t = half * TILES_DEV + (y + TILES_DEV - away) % TILES_DEV
            g_own[t] = landed[half]
            value_terms(t, landed[half])
    send_back(0, 0, v_got, 1.0)
    send_back(0, 1, v_got, 1.0)
    beside_arrived(1, v_side, v_all)
    each(0, OWN, output, 2)

    def own_values(u, _):
        dv_sum[u] = own_sum(u)
        return 0

    lax.fori_loop(0, OWN, own_values, 0)
    each(0, 2, backward, 2)
    finish(0, v_got, lambda u: dv_sum[u], dv_done)
    each(0, OWN, lambda t: send(3, dv_done, dv_out, t))
    each(2, TILES_DEV, backward, 2)
    send_back(1, 0, k_got, SCALE)
    each(TILES_DEV, OWN, backward, 2)
    send_back(1, 1, k_got, SCALE)
    each(0, OWN, query_grad, 2)
    finish(1, k_got, lambda u: own_sum(u) * SCALE, dk_done)
    each(0, OWN, lambda t: send(2, dk_done, dk_out, t))

    for copy in side_copies + list(back_copies.values()):
        copy.wait_send()
    for n, dst in enumerate((o_out, dq_out, dk_out, dv_out)):
        pltpu.make_async_copy(dst, dst, out_recv.at[n]).wait()
        most = dst.at[:, pl.ds(0, (HEADS - 1) * HD)]

        @pl.when(is_self)
        def _():
            pltpu.make_async_copy(most, most, in_send.at[n]).wait()
            pltpu.make_async_copy(most, most, out_send.at[n]).wait()

        @pl.when(jnp.logical_not(is_self))
        def _():
            pltpu.make_async_copy(dst, dst, in_send.at[n]).wait()
            pltpu.make_async_copy(dst, dst, out_send.at[n]).wait()


def hand_over(*refs):
    sources, results, (held, in_sem, out_sem) = refs[:4], refs[4:8], refs[8:]
    ins, outs = [], []
    for n in range(4):
        for i in range(2):
            part = pl.ds(i * HALF // 2, HALF // 2)
            ins.append(pltpu.make_async_copy(sources[n].at[part], held.at[n, part], in_sem.at[n, i]))
            outs.append(pltpu.make_async_copy(held.at[n, part], results[n].at[part], out_sem.at[n, i]))
    for copy in ins:
        copy.start()
    for arriving, leaving in zip(ins, outs):
        arriving.wait()
        leaving.start()
    for copy in outs:
        copy.wait()


def body(queries, keys, values, out_grad, block_list):
    hbm = pl.BlockSpec(memory_space=pl.ANY)
    dma = pltpu.SemaphoreType.DMA

    def tiles(*dims):
        return pltpu.VMEM((*dims, TILE, HD), jnp.bfloat16)

    def counts(*dims):
        return pltpu.SMEM(dims, jnp.int32)

    f32 = jnp.float32
    results = (jax.ShapeDtypeStruct((HALF, HEADS * HD), jnp.bfloat16),) * 4
    found = pl.pallas_call(
        kernel,
        out_shape=results,
        in_specs=[hbm] * 5,
        out_specs=(hbm,) * 4,
        scratch_shapes=[
            tiles(OWN), tiles(OWN), tiles(OWN), tiles(OWN),
            tiles(2), tiles(2), tiles(2), tiles(2),
            tiles(2 * SIDE), tiles(2 * SIDE), tiles(2, 2 * SIDE), tiles(SLOTS), tiles(SLOTS),
            pltpu.VMEM((MAXK, TILE, TILE), f32),
            pltpu.VMEM((OWN * MAXK, TILE, TILE), jnp.bfloat16),
            pltpu.VMEM((OWN, 1, TILE), f32),
            pltpu.VMEM((OWN, 1, TILE), f32),
            pltpu.VMEM((OWN * MAXK + 1, TILE, HD), f32),
            pltpu.VMEM((OWN, TILE, HD), f32),
            tiles(OWN), tiles(OWN), tiles(OWN), tiles(OWN),
            tiles(2, 2 * SIDE), tiles(2 * SIDE + 1), tiles(2 * SIDE + 1),
            counts(MAXK, 4 * GROUPS), counts(OWN, MAXK), counts(OWN), counts(OWN, OWN), counts(2 * SIDE, TILES_DEV),
            pltpu.SemaphoreType.DMA, dma((4,)), dma((3,)), dma((4,)), dma((4,)), dma((4,)),
            dma((2, 2)), dma((2, 2)), dma((2, 2, 2)), dma((2, 2, 2)),
        ],
        compiler_params=pltpu.CompilerParams(collective_id=0, has_side_effects=True, vmem_limit_bytes=VMEM_LIMIT),
    )(block_list.T, queries, keys, values, out_grad)
    return pl.pallas_call(
        hand_over,
        out_shape=results,
        in_specs=[hbm] * 4,
        out_specs=(hbm,) * 4,
        scratch_shapes=[pltpu.VMEM((4, HALF, HEADS * HD), jnp.bfloat16), dma((4, 2)), dma((4, 2))],
    )(*found)


def solution(mesh):
    tokens = P(("seq", "head"), None)
    return jax.shard_map(
        body,
        mesh=mesh,
        in_specs=(tokens, tokens, tokens, tokens, P()),
        out_specs=(tokens, tokens, tokens, tokens),
        check_vma=False,
    )
```

```python
import functools

import jax
import jax.numpy as jnp
from jax import lax
from jax.experimental import pallas as pl
from jax.experimental.pallas import tpu as pltpu
from jax.sharding import PartitionSpec as P

HD = 128
HEADS = 16
TILE = 384
HALF = TILE // 2
TILES_DEV = 4
MAXK = 7
GROUPS = 16
PAIRS = GROUPS // 2
OWN = 2 * TILES_DEV
SIDE = 6
SLOTS = OWN + 2 * SIDE
SCALE = HD**-0.5
LOG2E = 1.4426950408889634
MESH = pl.DeviceIdType.MESH
VMEM_LIMIT = 60 * 2**20


def place():
    seq, head = lax.axis_index("seq"), lax.axis_index("head")
    z, x_lo, core = seq // 4, (seq // 2) % 2, seq % 2
    y, x_hi = head // 2, head % 2
    return z, y, x_hi, x_lo, core


def device(z, y, x_hi, x_lo, core):
    return (z * 4 + x_lo * 2 + core, y * 2 + x_hi)


def sides():
    z, y, x_hi, x_lo, core = place()
    toward = 2 * core - 1
    pair = 2 * z + core
    near, far = 2 * pair + core, 2 * pair + 1 - core
    there = device((z + toward + 4) % 4, y, x_hi, x_lo, 1 - core)
    return there, device(z, y, x_hi, x_lo, 1 - core), near, far, toward


def turns(step, core):
    return jnp.where(step == 0, 2, jnp.where(step == 3, 0, jnp.where((step == 1) == (core == 0), 1, 3)))


def head_devices():
    z, y, x_hi, x_lo, core = place()
    found = []
    for dy in range(4):
        for dx in range(4):
            to_y, to_x = (y + dy) % 4, (2 * x_hi + x_lo + dx) % 4
            found.append((device(z, to_y, to_x // 2, to_x % 2, x_lo), to_y * 4 + to_x))
    return found


def token_devices():
    z, y, x_hi, x_lo, core = place()
    found = []
    for dy in range(4):
        for dx in range(2):
            for dc in range(2):
                at_y, at_x, at_core = (y + dy) % 4, (x_hi + dx) % 2, (core + dc) % 2
                found.append((device(z, at_y, at_x, core, at_core), at_core * 4 + at_y, at_x))
    return found


def greet(devices, is_self):
    barrier = pltpu.get_barrier_semaphore()
    for i, there in enumerate(devices):
        if i == 0:
            @pl.when(jnp.logical_not(is_self))
            def _():
                pl.semaphore_signal(barrier, inc=1, device_id=there, device_id_type=MESH)
        else:
            pl.semaphore_signal(barrier, inc=1, device_id=there, device_id_type=MESH)
    pl.semaphore_wait(barrier, len(devices) - is_self.astype(jnp.int32))


def listed(rows, seq, of):
    row0, tile0 = (seq + GROUPS) % GROUPS * TILES_DEV, of * TILES_DEV

    def one_row(r, found):
        low, high = found
        for m in range(MAXK):
            at = rows[m, row0 + r] - tile0
            inside = (at >= 0) & (at < TILES_DEV)
            low = jnp.minimum(low, jnp.where(inside, at, TILES_DEV))
            high = jnp.maximum(high, jnp.where(inside, at, -1))
        return low, high

    return lax.fori_loop(0, TILES_DEV, one_row, (jnp.int32(TILES_DEV), jnp.int32(-1)))


def asking(near, far, toward):
    mine = (
        (near, near + toward), (near, near + 2 * toward), (far, near + toward),
        (near, far - toward), (far, far - toward), (far, far - 2 * toward),
    )
    theirs = (
        (near + toward, near), (near + toward, far), (near + 2 * toward, near),
        (far - 2 * toward, far), (far - toward, far), (far - toward, near),
    )
    return mine, theirs


def dot(a, b, over_a, over_b):
    return lax.dot_general(a, b, (((over_a,), (over_b,)), ((), ())), preferred_element_type=jnp.float32)


def eights(x, op):
    return op(x.reshape(x.shape[0] // 8, 8, x.shape[1]), axis=0)


def fill_tables(rows, near, far, toward, mine, slot_of, count_of, own_from, side_from):
    first_tile = jnp.minimum(near, far) * TILES_DEV
    near_tile, far_tile = near * TILES_DEV - first_tile, far * TILES_DEV - first_tile
    lows = [listed(rows, seq, of)[0] for seq, of in mine]

    def find(t, _):
        is_near = t // TILES_DEV == near_tile // TILES_DEV
        count = jnp.int32(0)
        for m in range(MAXK):
            entry = rows[m, first_tile + t]
            valid = entry >= 0
            at = jnp.where(valid, entry, first_tile)
            away = (at // TILES_DEV - near) * toward
            inner = at % TILES_DEV
            slots = [2 * i + (inner != low).astype(jnp.int32) for i, low in enumerate(lows)]
            beside = jnp.where(
                away == 1,
                jnp.where(is_near, slots[0], slots[2]),
                jnp.where(away == 2, slots[1], jnp.where(away == -2, jnp.where(is_near, slots[3], slots[4]), slots[5])),
            )
            slot_of[t, m] = jnp.where((away == 0) | (away == -1), at - first_tile, OWN + beside)
            count = count + valid.astype(jnp.int32)
        count_of[t] = count
        return 0

    lax.fori_loop(0, OWN, find, 0)

    def where_listed(t, slot):
        found = jnp.int32(OWN * MAXK)
        count = count_of[t]
        for m in range(MAXK):
            found = jnp.where((slot_of[t, m] == slot) & (count > m), t * MAXK + m, found)
        return found

    def own(u, _):
        def one(t, _):
            own_from[u, t] = where_listed(t, u)
            return 0

        return lax.fori_loop(0, OWN, one, 0)

    lax.fori_loop(0, OWN, own, 0)

    def side(j, _):
        of_far = ((j >= 4) & (j < 6)) | (j >= 8)
        start = jnp.where(of_far, far_tile, near_tile)

        def one(i, _):
            side_from[j, i] = where_listed(start + i, OWN + j)
            return 0

        return lax.fori_loop(0, TILES_DEV, one, 0)

    lax.fori_loop(0, 2 * SIDE, side, 0)


def kernel(
    rows_in, q_in, k_in, v_in, g_in, o_out, dq_out, dk_out, dv_out,
    q_own, k_own, v_own, g_own, g_0, g_1, g_2, g_3, k_side, v_side, picked, k_all, v_all, score, expo, inv_of, delta_of, terms,
    own_part, o_done, dq_done, dk_done, dv_done, part, k_got, v_got,
    rows, slot_of, count_of, own_from, side_from,
    rows_sem, in_send, in_recv, part_recv, out_send, out_recv, side_send, side_recv, back_send, back_recv,
):
    z, y, x_hi, x_lo, core = place()
    is_self = x_lo == core
    z_side, core_side, near, far, toward = sides()
    mine, theirs = asking(near, far, toward)
    rows_copy = pltpu.make_async_copy(rows_in, rows, rows_sem)
    rows_copy.start()
    greet([d for d, _, _ in token_devices()] + [z_side, core_side], is_self)
    arrays = ((k_in, k_own), (q_in, q_own), (v_in, v_own), (g_in, g_own))
    tile, row = core * 4 + y, pl.multiple_of(x_hi * HALF, HALF)
    targets = head_devices()
    g_parts = (g_0, g_1, g_2, g_3)

    for n, (src, dst) in enumerate(arrays):
        for i, (there, head) in enumerate(targets):
            piece = src.at[:, pl.ds(pl.multiple_of(head * HD, HD), HD)]
            landing = g_parts[i // 4].at[core, pl.ds(row, HALF)] if n == 3 else dst.at[tile, pl.ds(row, HALF)]
            sem = part_recv.at[i // 4] if n == 3 else in_recv.at[n]
            if i == 0:
                @pl.when(is_self)
                def _():
                    pltpu.make_async_copy(piece, landing, sem).start()

                @pl.when(jnp.logical_not(is_self))
                def _():
                    pltpu.make_async_remote_copy(piece, landing, in_send.at[n], sem, there, MESH).start()
            else:
                pltpu.make_async_remote_copy(piece, landing, in_send.at[n], sem, there, MESH).start()

    def arrived(n):
        dst = arrays[n][1]
        pltpu.make_async_copy(dst, dst, in_recv.at[n]).wait()

    rows_copy.wait()
    fill_tables(rows, near, far, toward, mine, slot_of, count_of, own_from, side_from)
    near_tile, far_tile = core * TILES_DEV, (1 - core) * TILES_DEV
    asks = []
    for i, (seq, of) in enumerate(theirs):
        low, high = listed(rows, seq, of)
        asks.append((i in (0, 2, 5), 2 * i, low, high))
    terms[OWN * MAXK] = jnp.zeros((TILE, HD), jnp.float32)
    for got in (k_got, v_got):
        got[2 * SIDE] = jnp.zeros((TILE, HD), jnp.bfloat16)

    side_copies = []

    def to_sides(n, own, beside, whole):
        for of_near, slot, low, high in asks:
            start = near_tile if of_near else far_tile
            picked[n, slot] = own[start + jnp.minimum(low, TILES_DEV - 1)]
            picked[n, slot + 1] = own[start + jnp.maximum(high, 0)]
        for side, there in ((0, z_side), (1, core_side)):
            span = pl.ds(side * SIDE, SIDE)
            copy = pltpu.make_async_remote_copy(
                picked.at[n, span], beside.at[span], side_send.at[side, n], side_recv.at[side, n], there, MESH
            )
            copy.start()
            side_copies.append(copy)
        for u in range(OWN):
            whole[u] = own[u]

    def beside_arrived(n, beside, whole):
        for copy in side_copies[2 * n : 2 * n + 2]:
            copy.wait_recv()
        for j in range(2 * SIDE):
            whole[OWN + j] = beside[j]

    def tile_at(step):
        return ((core + step // TILES_DEV) % 2) * TILES_DEV + (y + turns(step % TILES_DEV, core)) % TILES_DEV

    head = y * 4 + 2 * x_hi + x_lo

    def send(n, src, dst, t):
        at_y, at_core = t % TILES_DEV, t // TILES_DEV
        for dx in range(2):
            at_x = (x_hi + dx) % 2
            there = device(z, at_y, at_x, core, at_core)
            piece = src.at[t, pl.ds(pl.multiple_of(at_x * HALF, HALF), HALF)]
            landing = dst.at[:, pl.ds(pl.multiple_of(head * HD, HD), HD)]
            remote = pltpu.make_async_remote_copy(piece, landing, out_send.at[n], out_recv.at[n], there, MESH)
            if dx == 0:
                here = is_self & (at_y == y) & (at_core == core)

                @pl.when(here)
                def _():
                    pltpu.make_async_copy(piece, landing, out_recv.at[n]).start()

                @pl.when(jnp.logical_not(here))
                def _():
                    remote.start()
            else:
                remote.start()

    def each(start, stop, do, by=1):
        def some(turn, _):
            for i in range(by):
                do(tile_at(start + turn * by + i))
            return 0

        lax.fori_loop(0, (stop - start) // by, some, 0)

    def weigh(t):
        q, count = q_own[t], count_of[t]
        top = jnp.full((8, TILE), -jnp.inf, jnp.float32)
        for m in range(MAXK):
            s = dot(k_all[slot_of[t, m]], q, 1, 1)
            score[m] = s
            top = jnp.maximum(top, jnp.where(count > m, eights(s, jnp.max), -jnp.inf))
        top = jnp.max(top, axis=0, keepdims=True)
        total = jnp.zeros((8, TILE), jnp.float32)
        for m in range(MAXK):
            e = jnp.exp2((score[m] - jnp.where(count > m, top, 1e30)) * (SCALE * LOG2E))
            expo[t * MAXK + m] = e.astype(jnp.bfloat16)
            total = total + eights(e, jnp.sum)
        inv_of[t] = 1.0 / jnp.sum(total, axis=0, keepdims=True)

    def row(t):
        return expo[pl.ds(t * MAXK, MAXK)].reshape(MAXK * TILE, TILE)

    def value_terms(t, g):
        g_scaled = (g.T.astype(jnp.float32) * inv_of[t]).astype(jnp.bfloat16)
        terms[pl.ds(t * MAXK, MAXK)] = dot(row(t), g_scaled, 1, 1).reshape(MAXK, TILE, HD)

    def output(t):
        out = jnp.zeros((HD, TILE), jnp.float32)
        for m in range(MAXK):
            out = out + dot(v_all[slot_of[t, m]], expo[t * MAXK + m], 0, 0)
        out = (out * inv_of[t]).astype(jnp.bfloat16)
        o_done[t] = out.T
        send(0, o_done, o_out, t)
        own_part[t] = own_sum(t)
        delta_of[t] = jnp.sum(g_own[t].T.astype(jnp.float32) * out.astype(jnp.float32), axis=0, keepdims=True)

    def backward(t):
        g, delta = g_own[t], delta_of[t]
        q_scaled = (q_own[t].T.astype(jnp.float32) * inv_of[t]).astype(jnp.bfloat16)
        for m in range(MAXK):
            dp = dot(v_all[slot_of[t, m]], g, 1, 1)
            ds = (expo[t * MAXK + m].astype(jnp.float32) * (dp - delta)).astype(jnp.bfloat16)
            expo[t * MAXK + m] = ds
        terms[pl.ds(t * MAXK, MAXK)] = dot(row(t), q_scaled, 1, 1).reshape(MAXK, TILE, HD)

    def query_grad(t):
        dq = jnp.zeros((HD, TILE), jnp.float32)
        for m in range(MAXK):
            dq = dq + dot(k_all[slot_of[t, m]], expo[t * MAXK + m], 0, 0)
        dq_done[t] = (dq * (inv_of[t] * SCALE)).astype(jnp.bfloat16).T
        send(1, dq_done, dq_out, t)
        own_part[t] = own_sum(t) * SCALE

    back_copies = {}

    def send_back(n, half, got, scale):
        def one(j, _):
            value = terms[side_from[j, 0]]
            for i in range(1, TILES_DEV):
                value = value + terms[side_from[j, i]]
            part[n, j] = (value * scale).astype(jnp.bfloat16)
            return 0

        for side, there, first, count in (((0, z_side, 0, 4), (1, core_side, 6, 2)), ((0, z_side, 4, 2), (1, core_side, 8, 4)))[half]:
            lax.fori_loop(first, first + count, one, 0)
            span = pl.ds(first, count)
            copy = pltpu.make_async_remote_copy(
                part.at[n, span], got.at[span], back_send.at[n, half, side], back_recv.at[n, half, side], there, MESH
            )
            copy.start()
            back_copies[n, half, side] = copy

    def own_sum(u):
        value = terms[own_from[u, 0]]
        for t in range(1, OWN):
            value = value + terms[own_from[u, t]]
        return value

    def finish(n, got, done, sent, out):
        for half in range(2):
            for side in range(2):
                back_copies[n, half, side].wait_recv()
        for step in range(OWN):
            t = tile_at(step)
            inner = t % TILES_DEV
            value = own_part[t]
            for of_near, slot, low, high in asks:
                if of_near == (step < TILES_DEV):
                    at = jnp.where(low == inner, slot, jnp.where(high == inner, slot + 1, 2 * SIDE))
                    value = value + got[at].astype(jnp.float32)
            done[t] = value.astype(jnp.bfloat16)
            send(sent, done, out, t)

    arrived(0)
    to_sides(0, k_own, k_side, k_all)
    beside_arrived(0, k_side, k_all)
    arrived(1)
    each(0, 5, weigh)
    arrived(2)
    to_sides(1, v_own, v_side, v_all)
    each(5, OWN, weigh)

    for away, landed in enumerate(g_parts):
        pltpu.make_async_copy(landed, landed, part_recv.at[away]).wait()
        for half in range(2):
            t = half * TILES_DEV + (y + TILES_DEV - away) % TILES_DEV
            g_own[t] = landed[half]
            value_terms(t, landed[half])
    send_back(0, 0, v_got, 1.0)
    send_back(0, 1, v_got, 1.0)
    beside_arrived(1, v_side, v_all)
    each(0, OWN, output, 2)

    each(0, 2, backward, 2)
    finish(0, v_got, dv_done, 3, dv_out)
    each(2, TILES_DEV, backward, 2)
    send_back(1, 0, k_got, SCALE)
    each(TILES_DEV, OWN, backward, 2)
    send_back(1, 1, k_got, SCALE)
    each(0, OWN, query_grad, 2)
    finish(1, k_got, dk_done, 2, dk_out)

    for copy in side_copies + list(back_copies.values()):
        copy.wait_send()
    for n, dst in enumerate((o_out, dq_out, dk_out, dv_out)):
        pltpu.make_async_copy(dst, dst, out_recv.at[n]).wait()
        most = dst.at[:, pl.ds(0, (HEADS - 1) * HD)]

        @pl.when(is_self)
        def _():
            pltpu.make_async_copy(most, most, in_send.at[n]).wait()
            pltpu.make_async_copy(most, most, out_send.at[n]).wait()

        @pl.when(jnp.logical_not(is_self))
        def _():
            pltpu.make_async_copy(dst, dst, in_send.at[n]).wait()
            pltpu.make_async_copy(dst, dst, out_send.at[n]).wait()


def hand_over(*refs):
    sources, results, (held, in_sem, out_sem) = refs[:4], refs[4:8], refs[8:]
    ins, outs = [], []
    for n in range(4):
        for i in range(2):
            part = pl.ds(i * HALF // 2, HALF // 2)
            ins.append(pltpu.make_async_copy(sources[n].at[part], held.at[n, part], in_sem.at[n, i]))
            outs.append(pltpu.make_async_copy(held.at[n, part], results[n].at[part], out_sem.at[n, i]))
    for copy in ins:
        copy.start()
    for arriving, leaving in zip(ins, outs):
        arriving.wait()
        leaving.start()
    for copy in outs:
        copy.wait()


def body(queries, keys, values, out_grad, block_list):
    hbm = pl.BlockSpec(memory_space=pl.ANY)
    dma = pltpu.SemaphoreType.DMA

    def tiles(*dims):
        return pltpu.VMEM((*dims, TILE, HD), jnp.bfloat16)

    def counts(*dims):
        return pltpu.SMEM(dims, jnp.int32)

    f32 = jnp.float32
    results = (jax.ShapeDtypeStruct((HALF, HEADS * HD), jnp.bfloat16),) * 4
    found = pl.pallas_call(
        kernel,
        out_shape=results,
        in_specs=[hbm] * 5,
        out_specs=(hbm,) * 4,
        scratch_shapes=[
            tiles(OWN), tiles(OWN), tiles(OWN), tiles(OWN),
            tiles(2), tiles(2), tiles(2), tiles(2),
            tiles(2 * SIDE), tiles(2 * SIDE), tiles(2, 2 * SIDE), tiles(SLOTS), tiles(SLOTS),
            pltpu.VMEM((MAXK, TILE, TILE), f32),
            pltpu.VMEM((OWN * MAXK, TILE, TILE), jnp.bfloat16),
            pltpu.VMEM((OWN, 1, TILE), f32),
            pltpu.VMEM((OWN, 1, TILE), f32),
            pltpu.VMEM((OWN * MAXK + 1, TILE, HD), f32),
            pltpu.VMEM((OWN, TILE, HD), f32),
            tiles(OWN), tiles(OWN), tiles(OWN), tiles(OWN),
            tiles(2, 2 * SIDE), tiles(2 * SIDE + 1), tiles(2 * SIDE + 1),
            counts(MAXK, 4 * GROUPS), counts(OWN, MAXK), counts(OWN), counts(OWN, OWN), counts(2 * SIDE, TILES_DEV),
            pltpu.SemaphoreType.DMA, dma((4,)), dma((3,)), dma((4,)), dma((4,)), dma((4,)),
            dma((2, 2)), dma((2, 2)), dma((2, 2, 2)), dma((2, 2, 2)),
        ],
        compiler_params=pltpu.CompilerParams(collective_id=0, has_side_effects=True, vmem_limit_bytes=VMEM_LIMIT),
    )(block_list.T, queries, keys, values, out_grad)
    return pl.pallas_call(
        hand_over,
        out_shape=results,
        in_specs=[hbm] * 4,
        out_specs=(hbm,) * 4,
        scratch_shapes=[pltpu.VMEM((4, HALF, HEADS * HD), jnp.bfloat16), dma((4, 2)), dma((4, 2))],
    )(*found)


def solution(mesh):
    tokens = P(("seq", "head"), None)
    return jax.shard_map(
        body,
        mesh=mesh,
        in_specs=(tokens, tokens, tokens, tokens, P()),
        out_specs=(tokens, tokens, tokens, tokens),
        check_vma=False,
    )
```

```python
import functools

import jax
import jax.numpy as jnp
from jax import lax
from jax.experimental import pallas as pl
from jax.experimental.pallas import tpu as pltpu
from jax.sharding import PartitionSpec as P

HD = 128
HEADS = 16
TILE = 384
HALF = TILE // 2
TILES_DEV = 4
MAXK = 7
GROUPS = 16
PAIRS = GROUPS // 2
OWN = 2 * TILES_DEV
SIDE = 6
SLOTS = OWN + 2 * SIDE
SCALE = HD**-0.5
LOG2E = 1.4426950408889634
MESH = pl.DeviceIdType.MESH
VMEM_LIMIT = 60 * 2**20


def place():
    seq, head = lax.axis_index("seq"), lax.axis_index("head")
    z, x_lo, core = seq // 4, (seq // 2) % 2, seq % 2
    y, x_hi = head // 2, head % 2
    return z, y, x_hi, x_lo, core


def device(z, y, x_hi, x_lo, core):
    return (z * 4 + x_lo * 2 + core, y * 2 + x_hi)


def sides():
    z, y, x_hi, x_lo, core = place()
    toward = 2 * core - 1
    pair = 2 * z + core
    near, far = 2 * pair + core, 2 * pair + 1 - core
    there = device((z + toward + 4) % 4, y, x_hi, x_lo, 1 - core)
    return there, device(z, y, x_hi, x_lo, 1 - core), near, far, toward


def turns(step, core):
    return jnp.where(step == 0, 2, jnp.where(step == 3, 0, jnp.where((step == 1) == (core == 0), 1, 3)))


def head_devices():
    z, y, x_hi, x_lo, core = place()
    found = []
    for dy in range(4):
        for dx in range(4):
            to_y, to_x = (y + dy) % 4, (2 * x_hi + x_lo + dx) % 4
            found.append((device(z, to_y, to_x // 2, to_x % 2, x_lo), to_y * 4 + to_x))
    return found


def token_devices():
    z, y, x_hi, x_lo, core = place()
    found = []
    for dy in range(4):
        for dx in range(2):
            for dc in range(2):
                at_y, at_x, at_core = (y + dy) % 4, (x_hi + dx) % 2, (core + dc) % 2
                found.append((device(z, at_y, at_x, core, at_core), at_core * 4 + at_y, at_x))
    return found


def greet(devices, is_self):
    barrier = pltpu.get_barrier_semaphore()
    for i, there in enumerate(devices):
        if i == 0:
            @pl.when(jnp.logical_not(is_self))
            def _():
                pl.semaphore_signal(barrier, inc=1, device_id=there, device_id_type=MESH)
        else:
            pl.semaphore_signal(barrier, inc=1, device_id=there, device_id_type=MESH)
    pl.semaphore_wait(barrier, len(devices) - is_self.astype(jnp.int32))


def listed(rows, seq, of):
    row0, tile0 = (seq + GROUPS) % GROUPS * TILES_DEV, of * TILES_DEV

    def one_row(r, found):
        low, high = found
        for m in range(MAXK):
            at = rows[m, row0 + r] - tile0
            inside = (at >= 0) & (at < TILES_DEV)
            low = jnp.minimum(low, jnp.where(inside, at, TILES_DEV))
            high = jnp.maximum(high, jnp.where(inside, at, -1))
        return low, high

    return lax.fori_loop(0, TILES_DEV, one_row, (jnp.int32(TILES_DEV), jnp.int32(-1)))


def asking(near, far, toward):
    mine = (
        (near, near + toward), (near, near + 2 * toward), (far, near + toward),
        (near, far - toward), (far, far - toward), (far, far - 2 * toward),
    )
    theirs = (
        (near + toward, near), (near + toward, far), (near + 2 * toward, near),
        (far - 2 * toward, far), (far - toward, far), (far - toward, near),
    )
    return mine, theirs


def dot(a, b, over_a, over_b):
    return lax.dot_general(a, b, (((over_a,), (over_b,)), ((), ())), preferred_element_type=jnp.float32)


def eights(x, op):
    return op(x.reshape(x.shape[0] // 8, 8, x.shape[1]), axis=0)


def fill_tables(rows, near, far, toward, mine, slot_of, count_of, own_from, side_from):
    first_tile = jnp.minimum(near, far) * TILES_DEV
    near_tile, far_tile = near * TILES_DEV - first_tile, far * TILES_DEV - first_tile
    lows = [listed(rows, seq, of)[0] for seq, of in mine]

    def find(t, _):
        is_near = t // TILES_DEV == near_tile // TILES_DEV
        count = jnp.int32(0)
        for m in range(MAXK):
            entry = rows[m, first_tile + t]
            valid = entry >= 0
            at = jnp.where(valid, entry, first_tile)
            away = (at // TILES_DEV - near) * toward
            inner = at % TILES_DEV
            slots = [2 * i + (inner != low).astype(jnp.int32) for i, low in enumerate(lows)]
            beside = jnp.where(
                away == 1,
                jnp.where(is_near, slots[0], slots[2]),
                jnp.where(away == 2, slots[1], jnp.where(away == -2, jnp.where(is_near, slots[3], slots[4]), slots[5])),
            )
            slot_of[t, m] = jnp.where((away == 0) | (away == -1), at - first_tile, OWN + beside)
            count = count + valid.astype(jnp.int32)
        count_of[t] = count
        return 0

    lax.fori_loop(0, OWN, find, 0)

    def where_listed(t, slot):
        found = jnp.int32(OWN * MAXK)
        count = count_of[t]
        for m in range(MAXK):
            found = jnp.where((slot_of[t, m] == slot) & (count > m), t * MAXK + m, found)
        return found

    def own(u, _):
        def one(t, _):
            own_from[u, t] = where_listed(t, u)
            return 0

        return lax.fori_loop(0, OWN, one, 0)

    lax.fori_loop(0, OWN, own, 0)

    def side(j, _):
        of_far = ((j >= 4) & (j < 6)) | (j >= 8)
        start = jnp.where(of_far, far_tile, near_tile)

        def one(i, _):
            side_from[j, i] = where_listed(start + i, OWN + j)
            return 0

        return lax.fori_loop(0, TILES_DEV, one, 0)

    lax.fori_loop(0, 2 * SIDE, side, 0)


def kernel(
    rows_in, q_in, k_in, v_in, g_in, o_out, dq_out, dk_out, dv_out,
    q_own, k_own, v_own, g_own, g_0, g_1, g_2, g_3, k_side, v_side, picked, k_all, v_all, score, expo, inv_of, delta_of, terms,
    own_part, o_done, dq_done, dk_done, dv_done, part, k_got, v_got,
    rows, slot_of, count_of, own_from, side_from,
    rows_sem, in_send, in_recv, part_recv, out_send, out_recv, side_send, side_recv, back_send, back_recv,
):
    z, y, x_hi, x_lo, core = place()
    is_self = x_lo == core
    z_side, core_side, near, far, toward = sides()
    mine, theirs = asking(near, far, toward)
    rows_copy = pltpu.make_async_copy(rows_in, rows, rows_sem)
    rows_copy.start()
    greet([d for d, _, _ in token_devices()] + [z_side, core_side], is_self)
    arrays = ((k_in, k_own), (q_in, q_own), (v_in, v_own), (g_in, g_own))
    tile, row = core * 4 + y, pl.multiple_of(x_hi * HALF, HALF)
    targets = head_devices()
    g_parts = (g_0, g_1, g_2, g_3)

    for n, (src, dst) in enumerate(arrays):
        for i, (there, head) in enumerate(targets):
            piece = src.at[:, pl.ds(pl.multiple_of(head * HD, HD), HD)]
            landing = g_parts[i // 4].at[core, pl.ds(row, HALF)] if n == 3 else dst.at[tile, pl.ds(row, HALF)]
            sem = part_recv.at[i // 4] if n == 3 else in_recv.at[n]
            if i == 0:
                @pl.when(is_self)
                def _():
                    pltpu.make_async_copy(piece, landing, sem).start()

                @pl.when(jnp.logical_not(is_self))
                def _():
                    pltpu.make_async_remote_copy(piece, landing, in_send.at[n], sem, there, MESH).start()
            else:
                pltpu.make_async_remote_copy(piece, landing, in_send.at[n], sem, there, MESH).start()

    def arrived(n):
        dst = arrays[n][1]
        pltpu.make_async_copy(dst, dst, in_recv.at[n]).wait()

    rows_copy.wait()
    fill_tables(rows, near, far, toward, mine, slot_of, count_of, own_from, side_from)
    near_tile, far_tile = core * TILES_DEV, (1 - core) * TILES_DEV
    asks = []
    for i, (seq, of) in enumerate(theirs):
        low, high = listed(rows, seq, of)
        asks.append((i in (0, 2, 5), 2 * i, low, high))
    terms[OWN * MAXK] = jnp.zeros((TILE, HD), jnp.float32)
    for got in (k_got, v_got):
        got[2 * SIDE] = jnp.zeros((TILE, HD), jnp.bfloat16)

    side_copies = []

    def to_sides(n, own, beside, whole):
        for of_near, slot, low, high in asks:
            start = near_tile if of_near else far_tile
            picked[n, slot] = own[start + jnp.minimum(low, TILES_DEV - 1)]
            picked[n, slot + 1] = own[start + jnp.maximum(high, 0)]
        for side, there in ((0, z_side), (1, core_side)):
            span = pl.ds(side * SIDE, SIDE)
            copy = pltpu.make_async_remote_copy(
                picked.at[n, span], beside.at[span], side_send.at[side, n], side_recv.at[side, n], there, MESH
            )
            copy.start()
            side_copies.append(copy)
        for u in range(OWN):
            whole[u] = own[u]

    def beside_arrived(n, beside, whole):
        for copy in side_copies[2 * n : 2 * n + 2]:
            copy.wait_recv()
        for j in range(2 * SIDE):
            whole[OWN + j] = beside[j]

    def tile_at(step):
        return ((core + step // TILES_DEV) % 2) * TILES_DEV + (y + turns(step % TILES_DEV, core)) % TILES_DEV

    head = y * 4 + 2 * x_hi + x_lo

    def send(n, src, dst, t):
        at_y, at_core = t % TILES_DEV, t // TILES_DEV
        for dx in range(2):
            at_x = (x_hi + dx) % 2
            there = device(z, at_y, at_x, core, at_core)
            piece = src.at[t, pl.ds(pl.multiple_of(at_x * HALF, HALF), HALF)]
            landing = dst.at[:, pl.ds(pl.multiple_of(head * HD, HD), HD)]
            remote = pltpu.make_async_remote_copy(piece, landing, out_send.at[n], out_recv.at[n], there, MESH)
            if dx == 0:
                here = is_self & (at_y == y) & (at_core == core)

                @pl.when(here)
                def _():
                    pltpu.make_async_copy(piece, landing, out_recv.at[n]).start()

                @pl.when(jnp.logical_not(here))
                def _():
                    remote.start()
            else:
                remote.start()

    def each(start, stop, do, by=1):
        def some(turn, _):
            for i in range(by):
                do(tile_at(start + turn * by + i))
            return 0

        lax.fori_loop(0, (stop - start) // by, some, 0)

    def weigh(t):
        q, count = q_own[t], count_of[t]
        top = jnp.full((8, TILE), -jnp.inf, jnp.float32)
        for m in range(MAXK):
            s = dot(k_all[slot_of[t, m]], q, 1, 1)
            score[m] = s
            top = jnp.maximum(top, jnp.where(count > m, eights(s, jnp.max), -jnp.inf))
        top = jnp.max(top, axis=0, keepdims=True)
        total = jnp.zeros((8, TILE), jnp.float32)
        for m in range(MAXK):
            e = jnp.exp2((score[m] - jnp.where(count > m, top, 1e30)) * (SCALE * LOG2E))
            expo[t * MAXK + m] = e.astype(jnp.bfloat16)
            total = total + eights(e, jnp.sum)
        inv_of[t] = 1.0 / jnp.sum(total, axis=0, keepdims=True)

    def row(t):
        return expo[pl.ds(t * MAXK, MAXK)].reshape(MAXK * TILE, TILE)

    def value_terms(t, g):
        g_scaled = (g.T.astype(jnp.float32) * inv_of[t]).astype(jnp.bfloat16)
        terms[pl.ds(t * MAXK, MAXK)] = dot(row(t), g_scaled, 1, 1).reshape(MAXK, TILE, HD)

    def output(t):
        out = jnp.zeros((HD, TILE), jnp.float32)
        for m in range(MAXK):
            out = out + dot(v_all[slot_of[t, m]], expo[t * MAXK + m], 0, 0)
        out = (out * inv_of[t]).astype(jnp.bfloat16)
        o_done[t] = out.T
        send(0, o_done, o_out, t)
        own_part[t] = own_sum(t)
        delta_of[t] = jnp.sum(g_own[t].T.astype(jnp.float32) * out.astype(jnp.float32), axis=0, keepdims=True)

    def backward(t):
        g, delta = g_own[t], delta_of[t]
        q_scaled = (q_own[t].T.astype(jnp.float32) * inv_of[t]).astype(jnp.bfloat16)
        for m in range(MAXK):
            dp = dot(v_all[slot_of[t, m]], g, 1, 1)
            ds = (expo[t * MAXK + m].astype(jnp.float32) * (dp - delta)).astype(jnp.bfloat16)
            expo[t * MAXK + m] = ds
        terms[pl.ds(t * MAXK, MAXK)] = dot(row(t), q_scaled, 1, 1).reshape(MAXK, TILE, HD)

    def query_grad(t):
        dq = jnp.zeros((HD, TILE), jnp.float32)
        for m in range(MAXK):
            dq = dq + dot(k_all[slot_of[t, m]], expo[t * MAXK + m], 0, 0)
        dq_done[t] = (dq * (inv_of[t] * SCALE)).astype(jnp.bfloat16).T
        send(1, dq_done, dq_out, t)

    back_copies = {}

    def send_back(n, half, got, scale):
        def one(j, _):
            value = terms[side_from[j, 0]]
            for i in range(1, TILES_DEV):
                value = value + terms[side_from[j, i]]
            part[n, j] = (value * scale).astype(jnp.bfloat16)
            return 0

        for side, there, first, count in (((0, z_side, 0, 4), (1, core_side, 6, 2)), ((0, z_side, 4, 2), (1, core_side, 8, 4)))[half]:
            lax.fori_loop(first, first + count, one, 0)
            span = pl.ds(first, count)
            copy = pltpu.make_async_remote_copy(
                part.at[n, span], got.at[span], back_send.at[n, half, side], back_recv.at[n, half, side], there, MESH
            )
            copy.start()
            back_copies[n, half, side] = copy

    def own_sum(u):
        value = terms[own_from[u, 0]]
        for t in range(1, OWN):
            value = value + terms[own_from[u, t]]
        return value

    def finish(n, got, done, sent, out):
        for half in range(2):
            for side in range(2):
                back_copies[n, half, side].wait_recv()
        for step in range(OWN):
            t = tile_at(step)
            inner = t % TILES_DEV
            value = own_part[t]
            for of_near, slot, low, high in asks:
                if of_near == (step < TILES_DEV):
                    at = jnp.where(low == inner, slot, jnp.where(high == inner, slot + 1, 2 * SIDE))
                    value = value + got[at].astype(jnp.float32)
            done[t] = value.astype(jnp.bfloat16)
            send(sent, done, out, t)

    arrived(0)
    to_sides(0, k_own, k_side, k_all)
    beside_arrived(0, k_side, k_all)
    arrived(1)
    each(0, 5, weigh)
    arrived(2)
    to_sides(1, v_own, v_side, v_all)
    each(5, OWN, weigh)

    for away, landed in enumerate(g_parts):
        pltpu.make_async_copy(landed, landed, part_recv.at[away]).wait()
        for half in range(2):
            t = half * TILES_DEV + (y + TILES_DEV - away) % TILES_DEV
            g_own[t] = landed[half]
            value_terms(t, landed[half])
    send_back(0, 0, v_got, 1.0)
    send_back(0, 1, v_got, 1.0)
    beside_arrived(1, v_side, v_all)
    each(0, OWN, output, 2)

    each(0, 2, backward, 2)
    finish(0, v_got, dv_done, 3, dv_out)
    each(2, TILES_DEV, backward, 2)
    send_back(1, 0, k_got, SCALE)
    each(0, TILES_DEV, query_grad, 2)
    each(TILES_DEV, OWN, backward, 2)
    send_back(1, 1, k_got, SCALE)
    each(TILES_DEV, OWN, query_grad, 2)

    def own_keys(u, _):
        own_part[u] = own_sum(u) * SCALE
        return 0

    lax.fori_loop(0, OWN, own_keys, 0)
    finish(1, k_got, dk_done, 2, dk_out)

    for copy in side_copies + list(back_copies.values()):
        copy.wait_send()
    for n, dst in enumerate((o_out, dq_out, dk_out, dv_out)):
        pltpu.make_async_copy(dst, dst, out_recv.at[n]).wait()
        most = dst.at[:, pl.ds(0, (HEADS - 1) * HD)]

        @pl.when(is_self)
        def _():
            pltpu.make_async_copy(most, most, in_send.at[n]).wait()
            pltpu.make_async_copy(most, most, out_send.at[n]).wait()

        @pl.when(jnp.logical_not(is_self))
        def _():
            pltpu.make_async_copy(dst, dst, in_send.at[n]).wait()
            pltpu.make_async_copy(dst, dst, out_send.at[n]).wait()


def hand_over(*refs):
    sources, results, (held, in_sem, out_sem) = refs[:4], refs[4:8], refs[8:]
    ins, outs = [], []
    for n in range(4):
        for i in range(2):
            part = pl.ds(i * HALF // 2, HALF // 2)
            ins.append(pltpu.make_async_copy(sources[n].at[part], held.at[n, part], in_sem.at[n, i]))
            outs.append(pltpu.make_async_copy(held.at[n, part], results[n].at[part], out_sem.at[n, i]))
    for copy in ins:
        copy.start()
    for arriving, leaving in zip(ins, outs):
        arriving.wait()
        leaving.start()
    for copy in outs:
        copy.wait()


def body(queries, keys, values, out_grad, block_list):
    hbm = pl.BlockSpec(memory_space=pl.ANY)
    dma = pltpu.SemaphoreType.DMA

    def tiles(*dims):
        return pltpu.VMEM((*dims, TILE, HD), jnp.bfloat16)

    def counts(*dims):
        return pltpu.SMEM(dims, jnp.int32)

    f32 = jnp.float32
    results = (jax.ShapeDtypeStruct((HALF, HEADS * HD), jnp.bfloat16),) * 4
    found = pl.pallas_call(
        kernel,
        out_shape=results,
        in_specs=[hbm] * 5,
        out_specs=(hbm,) * 4,
        scratch_shapes=[
            tiles(OWN), tiles(OWN), tiles(OWN), tiles(OWN),
            tiles(2), tiles(2), tiles(2), tiles(2),
            tiles(2 * SIDE), tiles(2 * SIDE), tiles(2, 2 * SIDE), tiles(SLOTS), tiles(SLOTS),
            pltpu.VMEM((MAXK, TILE, TILE), f32),
            pltpu.VMEM((OWN * MAXK, TILE, TILE), jnp.bfloat16),
            pltpu.VMEM((OWN, 1, TILE), f32),
            pltpu.VMEM((OWN, 1, TILE), f32),
            pltpu.VMEM((OWN * MAXK + 1, TILE, HD), f32),
            pltpu.VMEM((OWN, TILE, HD), f32),
            tiles(OWN), tiles(OWN), tiles(OWN), tiles(OWN),
            tiles(2, 2 * SIDE), tiles(2 * SIDE + 1), tiles(2 * SIDE + 1),
            counts(MAXK, 4 * GROUPS), counts(OWN, MAXK), counts(OWN), counts(OWN, OWN), counts(2 * SIDE, TILES_DEV),
            pltpu.SemaphoreType.DMA, dma((4,)), dma((3,)), dma((4,)), dma((4,)), dma((4,)),
            dma((2, 2)), dma((2, 2)), dma((2, 2, 2)), dma((2, 2, 2)),
        ],
        compiler_params=pltpu.CompilerParams(collective_id=0, has_side_effects=True, vmem_limit_bytes=VMEM_LIMIT),
    )(block_list.T, queries, keys, values, out_grad)
    return pl.pallas_call(
        hand_over,
        out_shape=results,
        in_specs=[hbm] * 4,
        out_specs=(hbm,) * 4,
        scratch_shapes=[pltpu.VMEM((4, HALF, HEADS * HD), jnp.bfloat16), dma((4, 2)), dma((4, 2))],
    )(*found)


def solution(mesh):
    tokens = P(("seq", "head"), None)
    return jax.shard_map(
        body,
        mesh=mesh,
        in_specs=(tokens, tokens, tokens, tokens, P()),
        out_specs=(tokens, tokens, tokens, tokens),
        check_vma=False,
    )
```
